128 devices in a mesh: ctx: 16 (over y, z), mp: 8 (over x, core).
Axes of the slice: x: 4, y: 4, z: 4, core: 2. Of those that a mesh axis runs over, the one named last changes fastest.
Arguments:
- block_entry_states: bfloat16 [16384, 2304], P('ctx'), may hold values from -6 to 6
- dispatch_preference: float32 [16384], P('ctx'), may hold values from -8 to 8
- chosen_positions: int32 [4096], P('ctx'), may hold values from 0 to 1023, as said below
- occupied_places: int32 [16], P('ctx'), may hold values from 64 to 256, as said below
- premix_rescaling_vector: float32 [2304], replicated, may hold values from 0.1 to 1.9
- asking_matrix: bfloat16 [2304, 4096], P(None, 'mp'), may hold values from -0.125 to 0.125
- lookup_matrix: bfloat16 [2304, 2048], P(None, 'mp'), may hold values from -0.125 to 0.125
- content_matrix: bfloat16 [2304, 2048], P(None, 'mp'), may hold values from -0.125 to 0.125
- final_mixing_matrix: bfloat16 [4096, 2304], P('mp'), may hold values from -0.09375 to 0.09375
- sharpness_coefficient: float32 [32], P('mp'), may hold values from 0.5 to 64
- premlp_rescaling_vector: float32 [2304], replicated, may hold values from 0.1 to 1.9
- switch_matrix: bfloat16 [2304, 18432], P('ctx', 'mp'), may hold values from -0.125 to 0.125
- expand_matrix: bfloat16 [2304, 18432], P('ctx', 'mp'), may hold values from -0.125 to 0.125
- contract_matrix: bfloat16 [2304, 18432], P('ctx', 'mp'), may hold values from -0.046875 to 0.046875
Outputs:
- residual_out: bfloat16 [16384, 2304], P('ctx')
The draws below stay inside these ranges and needn't reach their ends.
Inputs may be any that keep to these rules, and one draw needn't show every extreme that they name: `chosen_positions`: in each shard's block of 256 slots the first occupied_places entries are distinct positions within the shard in rising order; the remaining entries are other distinct positions of the shard and mean nothing. `occupied_places`: in every draw one shard has all 256 slots live.
All inputs are finite; a program needn't handle non-finite values.
Results may differ from the reference program's by a relative error of at most 0.0065.
Values may be sent and summed in bfloat16 or wider, within the bound.
No kernel may reach another device: no remote copies, remote signals or barrier semaphores. Data moves between devices by JAX's collectives and lax.ppermute only.
A program may use at most 128 MiB of HBM per device.

```python
import math
import jax
import jax.numpy as jnp
from jax import lax

D = 2304
HEADS = 32
KV_HEADS = 16
PER_HEAD_DIM = 128
FF = 18432
SEQ_DEV = 1024
CAP = 256
SEQ = 16384
SLOTS = 4096


def selection(key):
    shard_total = SEQ // SEQ_DEV
    count_key, index_key, full_key = jax.random.split(key, 3)
    counts = jax.random.randint(count_key, (shard_total,), CAP // 4, 3 * CAP // 4 + 1, dtype=jnp.int32)
    busiest = jax.random.randint(full_key, (), 0, shard_total, dtype=jnp.int32)
    counts = jnp.where(jnp.arange(shard_total, dtype=jnp.int32) == busiest, CAP, counts).astype(jnp.int32)

    def one_shard(shard_key, count):
        order = jax.random.permutation(shard_key, SEQ_DEV)[:CAP].astype(jnp.int32)
        slot_ids = jnp.arange(CAP, dtype=jnp.int32)
        ranked = jnp.sort(jnp.where(slot_ids < count, order, order + SEQ_DEV))
        return jnp.where(ranked >= SEQ_DEV, ranked - SEQ_DEV, ranked).astype(jnp.int32)
    picks = jax.vmap(one_shard)(jax.random.split(index_key, shard_total), counts)
    return (picks.reshape(-1), counts)


def draw_chosen_positions(key, part):
    picks, counts = selection(key)
    return picks


def draw_occupied_places(key, part):
    picks, counts = selection(key)
    return counts


def draw_sharpness_coefficient(key, part):
    key = jax.random.fold_in(key, 11)
    lowest, highest = (0.5, 2.0)
    fraction = jax.random.uniform(key, (HEADS,), jnp.float32)
    return jnp.exp(jnp.log(lowest) + fraction * jnp.log(highest / lowest)).astype(jnp.float32)


def steps_of(rng, dims, shards, least, high):
    level = 1.0
    for dim, shards_of in shards:
        draws = jax.random.uniform(jax.random.fold_in(jax.random.fold_in(rng, 6), dim), (shards_of,), jnp.float32, least / len(shards), high / len(shards))
        level = level * jnp.repeat(jnp.exp(draws), dims[dim] // shards_of).reshape((-1,) + (1,) * (len(dims) - 1 - dim))
    return level


def bell_draw(stream_key, extent, scale, most, pieces=(), held_as=jnp.bfloat16):
    drawn = scale * jax.random.normal(stream_key, extent, jnp.float32)
    if pieces:
        drawn = drawn * steps_of(stream_key, extent, pieces, -0.22, 0.18)
    return jnp.clip(drawn, -most, most).astype(held_as)


def setup_inputs(seed: int = 0) -> dict:
    streams_of = jax.random.split(jax.random.key(seed), 15)
    return {
        "block_entry_states": bell_draw(streams_of[0], (SEQ, D), 1.0, 6.0, ((0, 16),)),
        "dispatch_preference": bell_draw(streams_of[1], (SEQ,), 2.0, 8.0, ((0, 16),), jnp.float32),
        "chosen_positions": draw_chosen_positions(jax.random.fold_in(streams_of[14], 71), 0),
        "occupied_places": draw_occupied_places(jax.random.fold_in(streams_of[14], 71), 0),
        "premix_rescaling_vector": jnp.clip(1.0 + 0.18 * jax.random.normal(streams_of[4], (D,), jnp.float32), 0.1, 1.9),
        "asking_matrix": bell_draw(streams_of[5], (D, HEADS * PER_HEAD_DIM), D ** -0.5, 0.125, ((1, 8),)),
        "lookup_matrix": bell_draw(streams_of[6], (D, KV_HEADS * PER_HEAD_DIM), D ** -0.5, 0.125, ((1, 8),)),
        "content_matrix": bell_draw(streams_of[7], (D, KV_HEADS * PER_HEAD_DIM), D ** -0.5, 0.125, ((1, 8),)),
        "final_mixing_matrix": bell_draw(streams_of[8], (HEADS * PER_HEAD_DIM, D), (HEADS * PER_HEAD_DIM) ** -0.5, 0.09375, ((0, 8),)),
        "sharpness_coefficient": draw_sharpness_coefficient(jax.random.fold_in(streams_of[14], 71), 0),
        "premlp_rescaling_vector": jnp.clip(1.0 + 0.18 * jax.random.normal(streams_of[10], (D,), jnp.float32), 0.1, 1.9),
        "switch_matrix": bell_draw(streams_of[11], (D, FF), D ** -0.5, 0.125, ((0, 16), (1, 8))),
        "expand_matrix": bell_draw(streams_of[12], (D, FF), D ** -0.5, 0.125, ((0, 16), (1, 8))),
        "contract_matrix": bell_draw(streams_of[13], (D, FF), FF ** -0.5, 0.046875, ((0, 16), (1, 8))),
    }


epsilon = 1e-06
far_position = 1073741824

def normalize(inputs, scaling):
    values = inputs.astype(jnp.float32)
    dot_product_divisor = lax.rsqrt(lax.optimization_barrier(jnp.mean(values * values, axis=-1, keepdims=True)) + epsilon)
    return (values * dot_product_divisor * scaling).astype(jnp.bfloat16)

def rotate(values, positions):
    half_dim = values.shape[-1] // 2
    frequency = 10000.0 ** (-jnp.arange(half_dim, dtype=jnp.float32) / half_dim)
    angles = positions.astype(jnp.float32)[:, None] * frequency[None, :]
    cosine = jnp.cos(angles)[:, None, :]
    sine_part = jnp.sin(angles)[:, None, :]
    front_half = values[..., :half_dim]
    back_half = values[..., half_dim:]
    return jnp.concatenate([front_half * cosine - back_half * sine_part, back_half * cosine + front_half * sine_part], axis=-1)

def project(normed, weight, head_count, positions, turned):
    values = jnp.dot(normed, weight, preferred_element_type=jnp.float32)
    values = values.reshape(normed.shape[0], head_count, PER_HEAD_DIM)
    if turned:
        values = rotate(values, positions)
    return values.astype(jnp.bfloat16)

def reference(block_entry_states, dispatch_preference, chosen_positions, occupied_places, premix_rescaling_vector, asking_matrix, lookup_matrix, content_matrix, final_mixing_matrix, sharpness_coefficient, premlp_rescaling_vector, switch_matrix, expand_matrix, contract_matrix):
    slot_ids = jnp.arange(SLOTS, dtype=jnp.int32)
    shard_ids = slot_ids // CAP
    live_slot = slot_ids - shard_ids * CAP < occupied_places[shard_ids]
    positions = (shard_ids * SEQ_DEV + chosen_positions).astype(jnp.int32)
    key_position = jnp.where(live_slot, positions, far_position).astype(jnp.int32)
    picked = block_entry_states[positions]
    router_gate = jax.nn.sigmoid(dispatch_preference[positions].astype(jnp.float32))
    normed = normalize(picked, premix_rescaling_vector)
    queries = project(normed, asking_matrix, HEADS, positions, True)
    keys = project(normed, lookup_matrix, KV_HEADS, positions, True)
    values = project(normed, content_matrix, KV_HEADS, positions, False)
    askers_per_memory = HEADS // KV_HEADS
    asking_branch_matrix = queries.transpose(1, 0, 2)
    lookup_branch_matrix = jnp.repeat(keys, askers_per_memory, axis=1).transpose(1, 0, 2)
    content_branch_matrix = jnp.repeat(values, askers_per_memory, axis=1).transpose(1, 0, 2)
    allowed = key_position[None, :] <= positions[:, None]

    def branch_index(packed):
        query_one, key_one, value_one, scale_one = packed
        scores = jnp.dot(query_one, key_one.T, preferred_element_type=jnp.float32) * (scale_one / math.sqrt(PER_HEAD_DIM))
        scores = jnp.where(allowed, scores, -1e+30)
        row_max = lax.optimization_barrier(jnp.max(scores, axis=-1, keepdims=True))
        weights = jnp.exp(scores - row_max)
        row_sum = lax.optimization_barrier(jnp.sum(weights, axis=-1, keepdims=True))
        mixed_out = jnp.dot(weights.astype(jnp.bfloat16), value_one, preferred_element_type=jnp.float32) / row_sum
        return mixed_out.astype(jnp.bfloat16)
    per_branch_results = lax.map(branch_index, (asking_branch_matrix, lookup_branch_matrix, content_branch_matrix, sharpness_coefficient))
    per_branch_results = per_branch_results.transpose(1, 0, 2).reshape(SLOTS, HEADS * PER_HEAD_DIM)
    attention = jnp.dot(per_branch_results, final_mixing_matrix, preferred_element_type=jnp.float32)
    mid_state = (picked.astype(jnp.float32) + attention).astype(jnp.bfloat16)
    ffn_normed = normalize(mid_state, premlp_rescaling_vector)
    gate_act = jnp.dot(ffn_normed, switch_matrix, preferred_element_type=jnp.float32)
    up_act = jnp.dot(ffn_normed, expand_matrix, preferred_element_type=jnp.float32)
    hidden = (jax.nn.silu(gate_act) * up_act).astype(jnp.bfloat16)
    feed_out = lax.dot_general(hidden, contract_matrix, (((1,), (1,)), ((), ())), preferred_element_type=jnp.float32)
    result = (picked.astype(jnp.float32) + router_gate[:, None] * (attention + feed_out)).astype(jnp.bfloat16)
    target = jnp.where(live_slot, positions, SEQ).astype(jnp.int32)
    return block_entry_states.at[target].set(result, mode='drop')
```

```python
import functools
import math

import jax
import jax.numpy as jnp
from jax import lax
from jax.experimental import pallas as pl
from jax.experimental.pallas import tpu as pltpu
from jax.sharding import Mesh, PartitionSpec as P

D = 2304
CAP = 256
SEQ_DEV = 1024
HD = 128
FF_DEV = 1152
ROWS = 144
OWN = 32
EPS = 1e-06
NEG = -1e30
LOG2E = 1.4426950408889634
MB = 1024 * 1024
F32 = jnp.float32
BF16 = jnp.bfloat16


def vmem_spec():
    return pl.BlockSpec(memory_space=pltpu.VMEM)


def smem_spec():
    return pl.BlockSpec(memory_space=pltpu.SMEM)


def any_spec():
    return pl.BlockSpec(memory_space=pl.ANY)


def params(mib):
    return pltpu.CompilerParams(vmem_limit_bytes=mib * MB)


def project_body(info, block, chosen, gain, cosine, sine, wq_hbm, wk_hbm, wv_hbm,
                 q_out, kv_out, own_out, picked, normed, wq, wk, wv, sems):
    copies = [pltpu.make_async_copy(src, dst, sems.at[i])
              for i, (src, dst) in enumerate(((wq_hbm, wq), (wk_hbm, wk), (wv_hbm, wv)))]
    for copy in copies:
        copy.start()
    lanes = lax.broadcasted_iota(jnp.int32, (CAP, SEQ_DEV), 1)
    one_hot = jnp.where(lanes == chosen[...], 1.0, 0.0).astype(BF16)

    def pick(i, total):
        cols = pl.ds(pl.multiple_of(i * 256, 256), 256)
        part = jnp.dot(one_hot, block[:, cols], preferred_element_type=F32)
        picked[:, cols] = part.astype(BF16)
        return total + part * part

    total = lax.fori_loop(0, D // 256, pick, jnp.zeros((CAP, 256), F32))
    inv = lax.rsqrt(jnp.sum(total, axis=1, keepdims=True) / D + EPS)
    for i in range(D // 256):
        cols = slice(i * 256, (i + 1) * 256)
        normed[:, cols] = (picked[:, cols].astype(F32) * inv * gain[:, cols]).astype(BF16)
    own_out[...] = picked[pl.ds(pl.multiple_of(info[0], OWN), OWN), :]

    def turn(values):
        return values * cosine[...] + pltpu.roll(values, HD // 2, 1) * sine[...]

    copies[1].wait()
    keys = jnp.dot(normed[...], wk[...], preferred_element_type=F32)
    for h in range(2):
        kv_out[0:CAP, h * HD:(h + 1) * HD] = turn(keys[:, h * HD:(h + 1) * HD]).astype(BF16)
    copies[2].wait()
    kv_out[0:CAP, 256:512] = jnp.dot(normed[...], wv[...], preferred_element_type=F32).astype(BF16)
    kv_out[CAP:CAP + 16, :] = jnp.full((16, 512), info[1].astype(F32), F32).astype(BF16)
    copies[0].wait()
    for j in range(2):
        part = jnp.dot(normed[...], wq[:, j * 256:(j + 1) * 256], preferred_element_type=F32)
        for h in range(2):
            at = j * 256 + h * HD
            q_out[:, at:at + HD] = turn(part[:, h * HD:(h + 1) * HD]).astype(BF16)


def project(info, block, chosen, gain, cosine, sine, wq, wk, wv):
    return pl.pallas_call(
        project_body,
        out_shape=(jax.ShapeDtypeStruct((CAP, 512), BF16),
                   jax.ShapeDtypeStruct((CAP + 16, 512), BF16),
                   jax.ShapeDtypeStruct((OWN, D), BF16)),
        in_specs=[smem_spec()] + [vmem_spec()] * 5 + [any_spec()] * 3,
        out_specs=(vmem_spec(),) * 3,
        scratch_shapes=[pltpu.VMEM((CAP, D), BF16), pltpu.VMEM((CAP, D), BF16),
                        pltpu.VMEM((D, 512), BF16), pltpu.VMEM((D, 256), BF16),
                        pltpu.VMEM((D, 256), BF16), pltpu.SemaphoreType.DMA((3,))],
        compiler_params=params(28),
        name="project",
    )(info, block, chosen, gain, cosine, sine, wq, wk, wv)


def attend_body(diagonal, allow, scale, q, kv0, kv1, kv2, kv3, out, stats, values):
    kvs = (kv0, kv1, kv2, kv3)
    lane = lax.broadcasted_iota(jnp.int32, (1, CAP), 1).astype(F32)
    bias = []
    for j, kv in enumerate(kvs):
        count = kv[CAP:CAP + 16, 0:CAP].astype(F32)[0:1, :]
        live = (lane < count) & (allow[j] > 0)
        bias.append(jnp.where(live, 0.0, NEG))
    for g in range(2):
        for h in range(2):
            head = 2 * g + h
            for r in range(2):
                rows = slice(r * 128, (r + 1) * 128)
                query = q[rows, head * HD:(head + 1) * HD]
                scores = []
                for j, kv in enumerate(kvs):
                    part = lax.dot_general(query, kv[0:CAP, g * HD:(g + 1) * HD],
                                           (((1,), (1,)), ((), ())), preferred_element_type=F32)
                    part = part * scale[head] + bias[j]
                    if diagonal and j == 0:
                        slot = lax.broadcasted_iota(jnp.int32, (128, CAP), 0) + r * 128
                        key = lax.broadcasted_iota(jnp.int32, (128, CAP), 1)
                        part = jnp.where(key <= slot, part, NEG)
                    scores.append(part)
                top = functools.reduce(jnp.maximum, scores)
                top = jnp.max(top, axis=1, keepdims=True)
                total = jnp.zeros((128, CAP), F32)
                mixed = jnp.zeros((128, HD), F32)
                for j, kv in enumerate(kvs):
                    weight = jnp.exp2(scores[j] - top)
                    total = total + weight
                    mixed = mixed + jnp.dot(weight.astype(BF16),
                                            kv[0:CAP, 256 + g * HD:256 + (g + 1) * HD],
                                            preferred_element_type=F32)
                total = jnp.sum(total, axis=1, keepdims=True)
                out[rows, head * HD:(head + 1) * HD] = (mixed / total).astype(BF16)
                log_sum = top + jnp.log2(total)
                first = log_sum.astype(BF16).astype(F32)
                second = (log_sum - first).astype(BF16).astype(F32)
                third = log_sum - first - second
                stats[rows, head:head + 1] = first
                stats[rows, 4 + head:5 + head] = second
                stats[rows, 8 + head:9 + head] = third
    lanes = lax.broadcasted_iota(jnp.int32, (CAP, 128), 1)
    clean = jnp.where(lanes < 12, stats[...], 0.0)
    out[CAP:CAP + 16, 0:CAP] = jnp.transpose(clean)[0:16, :].astype(BF16)
    out[CAP:CAP + 16, CAP:512] = jnp.zeros((16, 512 - CAP), BF16)


def attend(diagonal, allow, scale, q, kvs):
    return pl.pallas_call(
        functools.partial(attend_body, diagonal),
        out_shape=jax.ShapeDtypeStruct((CAP + 16, 512), BF16),
        in_specs=[smem_spec(), smem_spec()] + [vmem_spec()] * 5,
        out_specs=vmem_spec(),
        scratch_shapes=[pltpu.VMEM((CAP, 128), F32), pltpu.VMEM((8, 128), F32)],
        compiler_params=params(16),
        name="attend",
    )(allow, scale, q, *kvs)


def mix_body(info, p0, p1, p2, p3, wo, keep, send, mixed):
    parts = (p0, p1, p2, p3)
    logs = []
    for part in parts:
        rows = part[CAP:CAP + 16, 0:CAP].astype(F32)
        rows = jnp.concatenate([rows, jnp.zeros((112, CAP), F32)], axis=0)
        logs.append(jnp.transpose(rows))
    for head in range(4):
        cols = slice(head * HD, (head + 1) * HD)
        each = [log[:, head:head + 1] + log[:, 4 + head:5 + head] + log[:, 8 + head:9 + head] for log in logs]
        top = functools.reduce(jnp.maximum, each)
        weights = [jnp.exp2(one - top) for one in each]
        total = functools.reduce(jnp.add, weights)
        value = functools.reduce(jnp.add, [w * part[0:CAP, cols].astype(F32) for w, part in zip(weights, parts)])
        mixed[:, cols] = (value / total).astype(BF16)
    core = info[2]
    mine = mixed[pl.ds(pl.multiple_of(core * 128, 128), 128), :]
    other = mixed[pl.ds(pl.multiple_of((1 - core) * 128, 128), 128), :]

    @pl.loop(0, D // 256)
    def _(i):
        cols = pl.ds(pl.multiple_of(i * 256, 256), 256)
        send[:, cols] = jnp.dot(other, wo[:, cols], preferred_element_type=F32).astype(BF16)
        keep[:, cols] = jnp.dot(mine, wo[:, cols], preferred_element_type=F32)


def mix(info, parts, wo):
    return pl.pallas_call(
        mix_body,
        out_shape=(jax.ShapeDtypeStruct((128, D), F32), jax.ShapeDtypeStruct((128, D), BF16)),
        in_specs=[smem_spec()] + [vmem_spec()] * 5,
        out_specs=(vmem_spec(),) * 2,
        scratch_shapes=[pltpu.VMEM((CAP, 512), BF16)],
        compiler_params=params(16),
        name="mix",
    )(info, *parts, wo)


def split_body(info, keep, got, own, s1, s2, s3):
    x = info[3]
    for d, ref in enumerate((own, s1, s2, s3)):
        rows = pl.ds(pl.multiple_of(lax.rem(x + d, 4) * OWN, OWN), OWN)
        ref[...] = (keep[rows, :] + got[rows, :].astype(F32)).astype(ref.dtype)


def split(info, keep, got):
    piece = jax.ShapeDtypeStruct((OWN, D), BF16)
    return pl.pallas_call(
        split_body,
        out_shape=(jax.ShapeDtypeStruct((OWN, D), F32), piece, piece, piece),
        in_specs=[smem_spec()] + [vmem_spec()] * 2,
        out_specs=(vmem_spec(),) * 4,
        compiler_params=params(16),
        name="split",
    )(info, keep, got)


def middle_body(picked, own, r1, r2, r3, gain, attention, normed):
    total = own[...] + r1[...].astype(F32) + r2[...].astype(F32) + r3[...].astype(F32)
    attention[...] = total
    mid = (picked[...].astype(F32) + total).astype(BF16).astype(F32)
    inv = lax.rsqrt(jnp.mean(mid * mid, axis=1, keepdims=True) + EPS)
    normed[...] = (mid * inv * gain[...]).astype(BF16)


def middle(picked, own, got, gain):
    return pl.pallas_call(
        middle_body,
        out_shape=(jax.ShapeDtypeStruct((OWN, D), F32), jax.ShapeDtypeStruct((OWN, D), BF16)),
        in_specs=[vmem_spec()] * 6,
        out_specs=(vmem_spec(),) * 2,
        compiler_params=params(16),
        name="middle",
    )(picked, own, *got, gain)


def feed_body(*refs):
    place = refs[0]
    xs = refs[1:17]
    pieces = refs[17:33]
    outs = refs[33:49]
    tokens, gate_up, down, hidden, sems = refs[49:]
    first = [pltpu.make_async_copy(piece.at[:, 0:D],
                                   gate_up.at[pl.ds(pl.multiple_of(place[i] * ROWS, 16), ROWS), :],
                                   sems.at[i])
             for i, piece in enumerate(pieces)]
    second = [pltpu.make_async_copy(piece.at[:, D:D + FF_DEV],
                                    down.at[pl.ds(pl.multiple_of(place[i] * ROWS, 16), ROWS), :],
                                    sems.at[16 + i])
              for i, piece in enumerate(pieces)]
    for copy in first + second:
        copy.start()
    for i, x in enumerate(xs):
        tokens[i * OWN:(i + 1) * OWN, :] = x[...]
    for copy in first:
        copy.wait()

    @pl.loop(0, FF_DEV // 128)
    def _(j):
        both = jnp.dot(tokens[...], gate_up[:, pl.ds(pl.multiple_of(j * 256, 256), 256)],
                       preferred_element_type=F32)
        gate = both[:, 0:128]
        up = both[:, 128:256]
        hidden[:, pl.ds(pl.multiple_of(j * 128, 128), 128)] = (
            gate / (1.0 + jnp.exp(-gate)) * up).astype(BF16)

    for copy in second:
        copy.wait()

    @pl.loop(0, D // 256)
    def _(n):
        rows = pl.ds(pl.multiple_of(n * 256, 256), 256)
        part = lax.dot_general(hidden[...], down[rows, :], (((1,), (1,)), ((), ())),
                               preferred_element_type=F32).astype(BF16)
        for i, out in enumerate(outs):
            out[:, rows] = part[i * OWN:(i + 1) * OWN, :]


def feed(place, xs, pieces):
    return pl.pallas_call(
        feed_body,
        out_shape=(jax.ShapeDtypeStruct((OWN, D), BF16),) * 16,
        in_specs=[smem_spec()] + [vmem_spec()] * 16 + [any_spec()] * 16,
        out_specs=(vmem_spec(),) * 16,
        scratch_shapes=[pltpu.VMEM((512, D), BF16), pltpu.VMEM((D, D), BF16),
                        pltpu.VMEM((D, FF_DEV), BF16), pltpu.VMEM((512, FF_DEV), BF16),
                        pltpu.SemaphoreType.DMA((32,))],
        compiler_params=params(36),
        name="feed",
    )(place, *xs, *pieces)


def finish_body(picked, attention, gate, *refs):
    total = attention[...]
    for ref in refs[:16]:
        total = total + ref[...].astype(F32)
    refs[16][...] = (picked[...].astype(F32) + gate[...] * total).astype(BF16)


def finish(picked, attention, gate, parts):
    return pl.pallas_call(
        finish_body,
        out_shape=jax.ShapeDtypeStruct((OWN, D), BF16),
        in_specs=[vmem_spec()] * 19,
        out_specs=vmem_spec(),
        compiler_params=params(16),
        name="finish",
    )(picked, attention, gate, *parts)


def place_body(info, chosen, block, *refs):
    pieces = refs[:8]
    out = refs[8]
    rows = refs[9]

    @pl.when(pl.program_id(0) == 0)
    def _():
        for i, piece in enumerate(pieces):
            rows[pl.ds(pl.multiple_of(info[8 + i] * OWN, OWN), OWN), :] = piece[...]

    position = lax.broadcasted_iota(jnp.int32, (128, CAP), 0) + pl.program_id(0) * 128
    slot = lax.broadcasted_iota(jnp.int32, (128, CAP), 1)
    hit = jnp.where((position == chosen[...]) & (slot < info[1]), 1.0, 0.0)
    taken = jnp.sum(hit, axis=1, keepdims=True) > 0.5
    hit = hit.astype(BF16)
    for n in range(D // 256):
        cols = slice(n * 256, (n + 1) * 256)
        new = jnp.dot(hit, rows[:, cols], preferred_element_type=F32).astype(BF16)
        out[:, cols] = jnp.where(taken, new, block[:, cols])


def put_back(info, chosen, block, pieces):
    return pl.pallas_call(
        place_body,
        grid=(SEQ_DEV // 128,),
        out_shape=jax.ShapeDtypeStruct((SEQ_DEV, D), BF16),
        in_specs=[smem_spec(), pl.BlockSpec((1, CAP), lambda i: (0, 0)),
                  pl.BlockSpec((128, D), lambda i: (i, 0))]
        + [pl.BlockSpec((OWN, D), lambda i: (0, 0))] * 8,
        out_specs=pl.BlockSpec((128, D), lambda i: (i, 0)),
        scratch_shapes=[pltpu.VMEM((CAP, D), BF16)],
        compiler_params=params(16),
        name="put_back",
    )(info, chosen, block, *pieces)


def shift(value, axis, step, size=4):
    return lax.ppermute(value, axis, [(i, (i + step) % size) for i in range(size)])


def shift2(value, dy, dx):
    pairs = [(4 * y + x, 4 * ((y + dy) % 4) + (x + dx) % 4) for y in range(4) for x in range(4)]
    return lax.ppermute(value, ("y", "x"), pairs)


def shift_mp(value, dx, dc):
    pairs = [(2 * x + c, 2 * ((x + dx) % 4) + (c + dc) % 2) for x in range(4) for c in range(2)]
    return lax.ppermute(value, ("x", "c"), pairs)


def weight_pieces(y, z, c, gate, up, down):
    packs = []
    for half in range(2):
        cols = slice(half * FF_DEV, (half + 1) * FF_DEV)
        both = jnp.stack([gate[:, cols].reshape(ROWS, 9, 128), up[:, cols].reshape(ROWS, 9, 128)], axis=2)
        packs.append(jnp.concatenate([both.reshape(ROWS, D), down[:, cols]], axis=1))
    got = []
    for s in range(2):
        pairs = []
        for sy in range(4):
            for sc in range(2):
                target = 2 * sc + (sy + s) % 2
                pairs.append((2 * sy + sc, 2 * target + sy // 2))
        send = jnp.where((y + s) % 2 == 0, packs[0], packs[1])
        got.append(lax.ppermute(send, ("y", "c"), pairs))
    ahead = [shift(piece, "z", 1) for piece in got]
    back = [shift(piece, "z", 3) for piece in got]
    far = [shift(ahead[0], "z", 1), shift(back[1], "z", 3)]
    mine = [(got, z), (ahead, (z + 3) % 4), (back, (z + 1) % 4), (far, (z + 2) % 4)]
    pieces, place = [], []
    for core in range(2):
        for four, source_z in mine:
            for s, piece in enumerate(four):
                if core == 0:
                    pieces.append(piece)
                    source_y = 2 * c + (y + s) % 2
                else:
                    pieces.append(shift(piece, "c", 1, 2))
                    source_y = 2 * (1 - c) + (y + s) % 2
                place.append(4 * source_y + source_z)
    return pieces, jnp.stack(place).astype(jnp.int32)


def local(block, preference, chosen, occupied, gain1, wq, wk, wv, wo, sharpness, gain2, gate_w, up_w, down_w):
    y, z, x, c = (lax.axis_index(n) for n in ("y", "z", "x", "c"))
    own_at = c * 128 + x * OWN
    order = [2 * 0 + 0] * 0
    for dx in range(4):
        for dc in range(2):
            order.append(((c + dc) % 2) * 4 + (x - dx) % 4)
    info = jnp.stack([own_at, occupied[0], c, x, y, z, y * 0, y * 0] + order).astype(jnp.int32)
    pieces, place = weight_pieces(y, z, c, gate_w, up_w, down_w)

    positions = (4 * y + z) * SEQ_DEV + chosen
    half = HD // 2
    frequency = 10000.0 ** (-jnp.arange(half, dtype=F32) / half)
    angles = positions.astype(F32)[:, None] * frequency[None, :]
    cosine, sine = jnp.cos(angles), jnp.sin(angles)
    cosine = jnp.concatenate([cosine, cosine], axis=1)
    sine = jnp.concatenate([-sine, sine], axis=1)
    q, kv, picked = project(info, block, chosen[:, None], gain1[None, :], cosine, sine, wq, wk, wv)

    kvs = [kv] + [shift(kv, "z", d) for d in (1, 2, 3)]
    scale = sharpness * (LOG2E / math.sqrt(HD))
    parts = []
    for d in (1, 2, 3):
        asked = shift(q, "y", d)
        allow = jnp.broadcast_to(((y - d) % 4 > y).astype(jnp.int32), (4,))
        parts.append(shift(attend(False, allow, scale, asked, kvs), "y", 4 - d))
    allow = jnp.stack([z >= 0] + [(z - d) % 4 < z for d in (1, 2, 3)]).astype(jnp.int32)
    parts.append(attend(True, allow, scale, q, kvs))

    keep, send = mix(info, parts, wo)
    own, s1, s2, s3 = split(info, keep, shift(send, "c", 1, 2))
    got = [shift(s, "x", d) for d, s in ((1, s1), (2, s2), (3, s3))]
    attention, normed = middle(picked, own, got, gain2[None, :])

    offsets = [(dy, dx) for dy in range(4) for dx in range(4)]
    xs = [normed] + [shift2(normed, dy, dx) for dy, dx in offsets[1:]]
    outs = feed(place, xs, pieces)
    back = [outs[0]] + [shift2(o, -dy, -dx) for o, (dy, dx) in zip(outs[1:], offsets[1:])]

    mine = lax.dynamic_slice_in_dim(chosen, own_at, OWN, 0)
    hit = mine[:, None] == jnp.arange(SEQ_DEV, dtype=jnp.int32)[None, :]
    router = jax.nn.sigmoid(jnp.sum(jnp.where(hit, preference[None, :], 0.0), axis=1, keepdims=True))
    result = finish(picked, attention, router, back)
    rows = [result if dx == 0 and dc == 0 else shift_mp(result, dx, dc) for dx in range(4) for dc in range(2)]
    return put_back(info, chosen[None, :], block, rows)


def solution(mesh):
    grid = Mesh(mesh.devices.reshape(4, 4, 4, 2), ("y", "z", "x", "c"))
    ctx, mp = ("y", "z"), ("x", "c")
    return jax.shard_map(
        local,
        mesh=grid,
        in_specs=(P(ctx, None), P(ctx), P(ctx), P(ctx), P(), P(None, mp), P(None, mp), P(None, mp),
                  P(mp, None), P(mp), P(), P(ctx, mp), P(ctx, mp), P(ctx, mp)),
        out_specs=P(ctx, None),
        check_vma=False,
    )
```

```python
import functools
import math

import jax
import jax.numpy as jnp
from jax import lax
from jax.experimental import pallas as pl
from jax.experimental.pallas import tpu as pltpu
from jax.sharding import Mesh, PartitionSpec as P

D = 2304
CAP = 256
SEQ_DEV = 1024
HD = 128
FF_DEV = 1152
ROWS = 144
STEP = 512
OWN = 32
EPS = 1e-06
NEG = -1e30
LOG2E = 1.4426950408889634
MB = 1024 * 1024
F32 = jnp.float32
BF16 = jnp.bfloat16


def vmem_spec():
    return pl.BlockSpec(memory_space=pltpu.VMEM)


def smem_spec():
    return pl.BlockSpec(memory_space=pltpu.SMEM)


def hbm_spec():
    return pl.BlockSpec(memory_space=pltpu.HBM)


def params(mib):
    return pltpu.CompilerParams(vmem_limit_bytes=mib * MB)


def begin_body(info, block_hbm, chosen, gain, frequency, wq_hbm, wk_hbm, wv_hbm,
               q_out, kv_out, own_out, block, picked, normed, wq, wk, wv, sems):
    tiles = D // 256
    loads = [pltpu.make_async_copy(block_hbm.at[:, i * 256:(i + 1) * 256],
                                   block.at[:, i * 256:(i + 1) * 256], sems.at[i])
             for i in range(tiles)]
    weights = [pltpu.make_async_copy(src, dst, sems.at[9 + i])
               for i, (src, dst) in enumerate(((wk_hbm, wk), (wv_hbm, wv), (wq_hbm, wq)))]
    for copy in loads + weights:
        copy.start()
    wide = jnp.broadcast_to(chosen[...].astype(F32), (128, CAP))
    column = jnp.transpose(wide)[:, 0:1].astype(jnp.int32)
    lanes = lax.broadcasted_iota(jnp.int32, (CAP, SEQ_DEV), 1)
    one_hot = jnp.where(lanes == column, 1.0, 0.0).astype(BF16)
    total = jnp.zeros((CAP, 256), F32)
    for i in range(tiles):
        cols = slice(i * 256, (i + 1) * 256)
        loads[i].wait()
        part = jnp.dot(one_hot, block[:, cols], preferred_element_type=F32)
        picked[:, cols] = part.astype(BF16)
        total = total + part * part
    angles = (column + info[6]).astype(F32) * frequency[...]
    cosine, sine = jnp.cos(angles), jnp.sin(angles)
    sine = jnp.where(lax.broadcasted_iota(jnp.int32, (CAP, HD), 1) < HD // 2, -sine, sine)
    inv = lax.rsqrt(jnp.sum(total, axis=1, keepdims=True) / D + EPS)
    for i in range(tiles):
        cols = slice(i * 256, (i + 1) * 256)
        normed[:, cols] = (picked[:, cols].astype(F32) * inv * gain[:, cols]).astype(BF16)
    own_out[...] = picked[pl.ds(pl.multiple_of(info[0], OWN), OWN), :]

    def turn(values):
        return values * cosine + pltpu.roll(values, HD // 2, 1) * sine

    weights[0].wait()
    keys = jnp.dot(normed[...], wk[...], preferred_element_type=F32)
    for h in range(2):
        kv_out[0:CAP, h * HD:(h + 1) * HD] = turn(keys[:, h * HD:(h + 1) * HD]).astype(BF16)
    weights[1].wait()
    kv_out[0:CAP, 256:512] = jnp.dot(normed[...], wv[...], preferred_element_type=F32).astype(BF16)
    kv_out[CAP:CAP + 16, :] = jnp.full((16, 512), info[1].astype(F32), F32).astype(BF16)
    weights[2].wait()
    for j in range(2):
        part = jnp.dot(normed[...], wq[:, j * 256:(j + 1) * 256], preferred_element_type=F32)
        for h in range(2):
            at = j * 256 + h * HD
            q_out[:, at:at + HD] = turn(part[:, h * HD:(h + 1) * HD]).astype(BF16)


def begin(info, block, chosen, gain, frequency, wq, wk, wv):
    return pl.pallas_call(
        begin_body,
        out_shape=(jax.ShapeDtypeStruct((CAP, 512), BF16), jax.ShapeDtypeStruct((CAP + 16, 512), BF16),
                   jax.ShapeDtypeStruct((OWN, D), BF16)),
        in_specs=[smem_spec(), hbm_spec()] + [vmem_spec()] * 3 + [hbm_spec()] * 3,
        out_specs=(vmem_spec(),) * 3,
        scratch_shapes=[pltpu.VMEM((SEQ_DEV, D), BF16), pltpu.VMEM((CAP, D), BF16), pltpu.VMEM((CAP, D), BF16),
                        pltpu.VMEM((D, 512), BF16), pltpu.VMEM((D, 256), BF16), pltpu.VMEM((D, 256), BF16),
                        pltpu.SemaphoreType.DMA((12,))],
        compiler_params=params(60),
        name="begin",
    )(info, block, chosen, gain, frequency, wq, wk, wv)


def pack_body(info, gate, up, down, out0, out1, packed, sems):
    loads, stores = [], []
    for s, out in enumerate((out0, out1)):
        cols = pl.ds(pl.multiple_of(lax.rem(info[4] + s, 2) * FF_DEV, FF_DEV), FF_DEV)
        for k, weight in enumerate((gate, up, down)):
            rows = slice(k * ROWS, (k + 1) * ROWS)
            at = 3 * s + k
            loads.append(pltpu.make_async_copy(weight.at[:, cols], packed.at[s, rows, :], sems.at[at]))
            stores.append(pltpu.make_async_copy(packed.at[s, rows, :], out.at[rows, :], sems.at[6 + at]))
    for load in loads:
        load.start()
    for load, store in zip(loads, stores):
        load.wait()
        store.start()
    for store in stores:
        store.wait()


def pack(info, gate, up, down):
    return pl.pallas_call(
        pack_body,
        out_shape=(jax.ShapeDtypeStruct((3 * ROWS, FF_DEV), BF16),) * 2,
        in_specs=[smem_spec()] + [hbm_spec()] * 3,
        out_specs=(hbm_spec(),) * 2,
        scratch_shapes=[pltpu.VMEM((2, 3 * ROWS, FF_DEV), BF16), pltpu.SemaphoreType.DMA((12,))],
        compiler_params=params(60),
        name="pack",
    )(info, gate, up, down)


def attend_body(diagonal, at, scale, q, kv0, kv1, kv2, kv3, out, stats, turned):
    lane = lax.broadcasted_iota(jnp.int32, (1, CAP), 1).astype(F32)
    bias = []
    kvs = (kv0, kv1, kv2, kv3)
    for j, kv in enumerate(kvs):
        count = kv[CAP:CAP + 16, 0:CAP].astype(F32)[0:1, :]
        live = (lane < count) & (at[j] >= 0)
        bias.append(jnp.where(live, 0.0, NEG))
        for g in range(2):
            turned[g * HD:(g + 1) * HD, j * CAP:(j + 1) * CAP] = jnp.transpose(kv[0:CAP, g * HD:(g + 1) * HD])
    past = lax.broadcasted_iota(jnp.int32, (CAP, CAP), 1) - lax.broadcasted_iota(jnp.int32, (CAP, CAP), 0)
    for head in range(4):
        g = head // 2
        cols = slice(head * HD, (head + 1) * HD)
        query = q[:, cols]
        scores = []
        for j in range(4):
            part = jnp.dot(query, turned[g * HD:(g + 1) * HD, j * CAP:(j + 1) * CAP],
                           preferred_element_type=F32)
            part = part * scale[head] + bias[j]
            if diagonal:
                part = jnp.where(past <= at[j], part, NEG)
            scores.append(part)
        top = jnp.max(functools.reduce(jnp.maximum, scores), axis=1, keepdims=True)
        weights = [jnp.exp2(part - top) for part in scores]
        total = jnp.sum(functools.reduce(jnp.add, weights), axis=1, keepdims=True)
        mixed = jnp.zeros((CAP, HD), F32)
        for j, kv in enumerate(kvs):
            mixed = mixed + jnp.dot(weights[j].astype(BF16), kv[0:CAP, 256 + g * HD:256 + (g + 1) * HD],
                                    preferred_element_type=F32)
        out[0:CAP, cols] = (mixed * (1.0 / total)).astype(BF16)
        log_sum = top + jnp.log2(total)
        first = log_sum.astype(BF16).astype(F32)
        second = (log_sum - first).astype(BF16).astype(F32)
        stats[:, head:head + 1] = first
        stats[:, 4 + head:5 + head] = second
        stats[:, 8 + head:9 + head] = log_sum - first - second
    lanes = lax.broadcasted_iota(jnp.int32, (CAP, 128), 1)
    clean = jnp.where(lanes < 12, stats[...], 0.0)
    out[CAP:CAP + 16, 0:CAP] = jnp.transpose(clean)[0:16, :].astype(BF16)
    out[CAP:CAP + 16, CAP:512] = jnp.zeros((16, 512 - CAP), BF16)


def attend(diagonal, at, scale, q, kvs):
    return pl.pallas_call(
        functools.partial(attend_body, diagonal),
        out_shape=jax.ShapeDtypeStruct((CAP + 16, 512), BF16),
        in_specs=[smem_spec()] * 2 + [vmem_spec()] * 5,
        out_specs=vmem_spec(),
        scratch_shapes=[pltpu.VMEM((CAP, 128), F32), pltpu.VMEM((256, 1024), BF16)],
        compiler_params=params(12),
        name="attend",
    )(at, scale, q, *kvs)


def mix_body(info, p0, p1, p2, p3, wo, keep, send, mixed):
    parts = (p0, p1, p2, p3)
    logs = []
    for part in parts:
        rows = part[CAP:CAP + 16, 0:CAP].astype(F32)
        rows = jnp.concatenate([rows, jnp.zeros((112, CAP), F32)], axis=0)
        logs.append(jnp.transpose(rows))
    for head in range(4):
        cols = slice(head * HD, (head + 1) * HD)
        each = [log[:, head:head + 1] + log[:, 4 + head:5 + head] + log[:, 8 + head:9 + head] for log in logs]
        top = functools.reduce(jnp.maximum, each)
        weights = [jnp.exp2(one - top) for one in each]
        total = functools.reduce(jnp.add, weights)
        value = functools.reduce(jnp.add, [w * part[0:CAP, cols].astype(F32) for w, part in zip(weights, parts)])
        mixed[:, cols] = (value / total).astype(BF16)
    core = info[2]
    mine = mixed[pl.ds(pl.multiple_of(core * 128, 128), 128), :]
    other = mixed[pl.ds(pl.multiple_of((1 - core) * 128, 128), 128), :]

    @pl.loop(0, D // 256)
    def _(i):
        cols = pl.ds(pl.multiple_of(i * 256, 256), 256)
        send[:, cols] = jnp.dot(other, wo[:, cols], preferred_element_type=F32).astype(BF16)
        keep[:, cols] = jnp.dot(mine, wo[:, cols], preferred_element_type=F32)


def mix(info, parts, wo):
    return pl.pallas_call(
        mix_body,
        out_shape=(jax.ShapeDtypeStruct((128, D), F32), jax.ShapeDtypeStruct((128, D), BF16)),
        in_specs=[smem_spec()] + [vmem_spec()] * 5,
        out_specs=(vmem_spec(),) * 2,
        scratch_shapes=[pltpu.VMEM((CAP, 512), BF16)],
        compiler_params=params(12),
        name="mix",
    )(info, *parts, wo)


def split_body(info, keep, got, own, s1, s2, s3):
    x = info[3]
    for d, ref in enumerate((own, s1, s2, s3)):
        rows = pl.ds(pl.multiple_of(lax.rem(x + d, 4) * OWN, OWN), OWN)
        ref[...] = (keep[rows, :] + got[rows, :].astype(F32)).astype(ref.dtype)


def split(info, keep, got):
    piece = jax.ShapeDtypeStruct((OWN, D), BF16)
    return pl.pallas_call(
        split_body,
        out_shape=(jax.ShapeDtypeStruct((OWN, D), F32), piece, piece, piece),
        in_specs=[smem_spec()] + [vmem_spec()] * 2,
        out_specs=(vmem_spec(),) * 4,
        compiler_params=params(12),
        name="split",
    )(info, keep, got)


def middle_body(picked, own, r1, r2, r3, gain, attention, normed):
    total = own[...] + r1[...].astype(F32) + r2[...].astype(F32) + r3[...].astype(F32)
    attention[...] = total
    mid = (picked[...].astype(F32) + total).astype(BF16).astype(F32)
    inv = lax.rsqrt(jnp.mean(mid * mid, axis=1, keepdims=True) + EPS)
    normed[...] = (mid * inv * gain[...]).astype(BF16)


def middle(picked, own, got, gain):
    return pl.pallas_call(
        middle_body,
        out_shape=(jax.ShapeDtypeStruct((OWN, D), F32), jax.ShapeDtypeStruct((OWN, D), BF16)),
        in_specs=[vmem_spec()] * 6,
        out_specs=(vmem_spec(),) * 2,
        compiler_params=params(12),
        name="middle",
    )(picked, own, *got, gain)


def feed_body(*refs):
    place = refs[0]
    xs = refs[1:5]
    pieces = refs[5:13]
    outs = refs[13:17]
    tokens, gate, up, down, hidden, sems = refs[17:]
    copies = [[], [], []]
    for e, x in enumerate(xs):
        copies[0].append(pltpu.make_async_copy(x, tokens.at[e * 128:(e + 1) * 128, :], sems.at[e]))
    for k, weight in enumerate((gate, up, down)):
        for i in range(16):
            rows = pl.ds(pl.multiple_of(place[i] * ROWS, 16), ROWS)
            at = (3 * (i % 2) + k) * ROWS
            copies[k].append(pltpu.make_async_copy(pieces[i // 2].at[at:at + ROWS, :], weight.at[rows, :],
                                                   sems.at[4 + 16 * k + i]))
    for copy in copies[0] + copies[1] + copies[2]:
        copy.start()
    for copy in copies[0]:
        copy.wait()
    chunks = [slice(j * 256, min((j + 1) * 256, FF_DEV)) for j in range(5)]
    for j, cols in enumerate(chunks):
        one = jnp.dot(tokens[...], gate[:, cols], preferred_element_type=F32)
        if j == 0:
            for copy in copies[1]:
                copy.wait()
        two = jnp.dot(tokens[...], up[:, cols], preferred_element_type=F32)
        hidden[:, cols] = (one / (1.0 + jnp.exp(-one)) * two).astype(BF16)
    for copy in copies[2]:
        copy.wait()
    for n in range(D // 256):
        rows = slice(n * 256, (n + 1) * 256)
        part = lax.dot_general(hidden[...], down[rows, :], (((1,), (1,)), ((), ())),
                               preferred_element_type=F32).astype(BF16)
        for e, out in enumerate(outs):
            out[:, rows] = part[e * 128:(e + 1) * 128, :]


def feed(place, xs, pieces):
    return pl.pallas_call(
        feed_body,
        out_shape=(jax.ShapeDtypeStruct((4 * OWN, D), BF16),) * 4,
        in_specs=[smem_spec()] + [hbm_spec()] * 12,
        out_specs=(vmem_spec(),) * 4,
        scratch_shapes=[pltpu.VMEM((512, D), BF16), pltpu.VMEM((D, FF_DEV), BF16), pltpu.VMEM((D, FF_DEV), BF16),
                        pltpu.VMEM((D, FF_DEV), BF16), pltpu.VMEM((512, FF_DEV), BF16),
                        pltpu.SemaphoreType.DMA((52,))],
        compiler_params=params(60),
        name="feed",
    )(place, *xs, *pieces)


def fold_body(p0, p1, p2, p3, own, s1, s2, s3):
    for d, out in enumerate((own, s1, s2, s3)):
        rows = slice(d * OWN, (d + 1) * OWN)
        total = p0[rows, :].astype(F32) + p1[rows, :].astype(F32)
        out[...] = (total + p2[rows, :].astype(F32) + p3[rows, :].astype(F32)).astype(out.dtype)


def fold(parts):
    piece = jax.ShapeDtypeStruct((OWN, D), BF16)
    return pl.pallas_call(
        fold_body,
        out_shape=(jax.ShapeDtypeStruct((OWN, D), F32), piece, piece, piece),
        in_specs=[vmem_spec()] * 4,
        out_specs=(vmem_spec(),) * 4,
        compiler_params=params(12),
        name="fold",
    )(*parts)


def finish_body(picked, attention, gate, own, r1, r2, r3, out):
    total = attention[...] + own[...]
    total = total + r1[...].astype(F32) + r2[...].astype(F32) + r3[...].astype(F32)
    out[...] = (picked[...].astype(F32) + gate[...] * total).astype(BF16)


def finish(picked, attention, gate, parts):
    return pl.pallas_call(
        finish_body,
        out_shape=jax.ShapeDtypeStruct((OWN, D), BF16),
        in_specs=[vmem_spec()] * 7,
        out_specs=vmem_spec(),
        compiler_params=params(12),
        name="finish",
    )(picked, attention, gate, *parts)


def merge_body(first, second, out, sems):
    copies = [pltpu.make_async_copy(ref, out.at[s * 3 * ROWS:(s + 1) * 3 * ROWS, :], sems.at[s])
              for s, ref in enumerate((first, second))]
    for copy in copies:
        copy.start()
    for copy in copies:
        copy.wait()


def merge(first, second):
    return pl.pallas_call(
        merge_body,
        out_shape=jax.ShapeDtypeStruct((6 * ROWS, FF_DEV), BF16),
        in_specs=[hbm_spec()] * 2,
        out_specs=vmem_spec(),
        scratch_shapes=[pltpu.SemaphoreType.DMA((2,))],
        compiler_params=params(60),
        name="merge",
    )(first, second)


def join_body(*refs):
    for i, ref in enumerate(refs[:4]):
        refs[4][i * OWN:(i + 1) * OWN, :] = ref[...]


def join(pieces):
    return pl.pallas_call(
        join_body,
        out_shape=jax.ShapeDtypeStruct((4 * OWN, D), BF16),
        in_specs=[vmem_spec()] * 4,
        out_specs=vmem_spec(),
        compiler_params=params(12),
        name="join",
    )(*pieces)


def place_body(info, chosen, block, *refs):
    pieces = refs[:2]
    out = refs[2]
    rows = refs[3]

    @pl.when(pl.program_id(0) == 0)
    def _():
        for core, piece in enumerate(pieces):
            for dx in range(4):
                at = lax.rem(info[2] + core, 2) * 128 + lax.rem(info[3] + 4 - dx, 4) * OWN
                rows[pl.ds(pl.multiple_of(at, OWN), OWN), :] = piece[dx * OWN:(dx + 1) * OWN, :]

    position = lax.broadcasted_iota(jnp.int32, (STEP, CAP), 0) + pl.program_id(0) * STEP
    slot = lax.broadcasted_iota(jnp.int32, (STEP, CAP), 1)
    hit = jnp.where((position == chosen[...]) & (slot < info[1]), 1.0, 0.0)
    taken = jnp.sum(hit, axis=1, keepdims=True) > 0.5
    hit = hit.astype(BF16)
    for n in range(D // 256):
        cols = slice(n * 256, (n + 1) * 256)
        new = jnp.dot(hit, rows[:, cols], preferred_element_type=F32).astype(BF16)
        out[:, cols] = jnp.where(taken, new, block[:, cols])


def put_back(info, chosen, block, pieces):
    return pl.pallas_call(
        place_body,
        grid=(SEQ_DEV // STEP,),
        out_shape=jax.ShapeDtypeStruct((SEQ_DEV, D), BF16),
        in_specs=[smem_spec(), pl.BlockSpec((1, CAP), lambda i: (0, 0)),
                  pl.BlockSpec((STEP, D), lambda i: (i, 0))]
        + [pl.BlockSpec((128, D), lambda i: (0, 0))] * 2,
        out_specs=pl.BlockSpec((STEP, D), lambda i: (i, 0)),
        scratch_shapes=[pltpu.VMEM((CAP, D), BF16)],
        compiler_params=params(60),
        name="put_back",
    )(info, chosen, block, *pieces)


def shift(value, axis, step, size=4):
    return lax.ppermute(value, axis, [(i, (i + step) % size) for i in range(size)])


def cross(value, step, first):
    pairs = []
    for y in range(4):
        for x in range(4):
            for c in range(2):
                along_x = (c == 0) == first
                to_y, to_x = (y, (x + step) % 4) if along_x else ((y + step) % 4, x)
                pairs.append((8 * y + 2 * x + c, 8 * to_y + 2 * to_x + c))
    return lax.ppermute(value, ("y", "x", "c"), pairs)


def around(value, step):
    pairs = [(2 * z + c, 2 * ((z + (step if c == 0 else 4 - step)) % 4) + c) for z in range(4) for c in range(2)]
    return lax.ppermute(value, ("z", "c"), pairs)


def swap(value):
    return shift(value, "c", 1, 2)


def weight_pairs(s):
    return [(2 * sy + sc, 2 * (2 * sc + (sy + s) % 2) + sy // 2) for sy in range(4) for sc in range(2)]


def tie(*values):
    return lax.optimization_barrier(values)


def local(block, preference, chosen, occupied, gain1, wq, wk, wv, wo, sharpness, gain2, gate_w, up_w, down_w):
    y, z, x, c = (lax.axis_index(n) for n in ("y", "z", "x", "c"))
    own_at = c * 128 + x * OWN
    info = jnp.stack([own_at, occupied[0], c, x, y, z, (4 * y + z) * SEQ_DEV]).astype(jnp.int32)
    near = 3 - 2 * c
    place = []
    for core, step in ((c, near), (1 - c, 4 - near)):
        for source in (z, z + step, z + 4 - step, z + 2):
            for s in range(2):
                place.append(4 * (2 * core + (y + s) % 2) + source % 4)
    place = jnp.stack(place).astype(jnp.int32)

    half = HD // 2
    frequency = 10000.0 ** (-jnp.arange(half, dtype=F32) / half)
    frequency = jnp.concatenate([frequency, frequency])[None, :]
    packs = pack(info, gate_w, up_w, down_w)
    *packs, info = tie(*packs, info)
    got = [lax.ppermute(p, ("y", "c"), weight_pairs(s)) for s, p in enumerate(packs)]
    q, kv, picked = begin(info, block, chosen[None, :], gain1[None, :], frequency, wq, wk, wv)

    kvs = [kv] + [shift(kv, "z", d) for d in (1, 2, 3)]
    q, *got = tie(q, *got)
    asked = [shift(q, "y", d) for d in (1, 2, 3)]
    merged = merge(*got)
    *kvs, merged = tie(*kvs, merged)
    near, side = around(merged, 1), around(merged, 3)

    scale = sharpness * (LOG2E / math.sqrt(HD))
    parts = []
    for d in (1, 2, 3):
        at = jnp.broadcast_to(jnp.where((y - d) % 4 > y, CAP, -CAP), (4,)).astype(jnp.int32)
        parts.append(shift(attend(False, at, scale, asked[d - 1], kvs), "y", 4 - d))
    at = jnp.stack([z * 0] + [jnp.where(z >= d, CAP, -CAP) for d in (1, 2, 3)]).astype(jnp.int32)
    parts.append(attend(True, at, scale, q, kvs))

    keep, send = mix(info, parts, wo)
    met, near = tie(swap(send), near)
    far = around(near, 1)
    own, s1, s2, s3 = split(info, keep, met)
    moved = [shift(s, "x", d) for d, s in ((1, s1), (2, s2), (3, s3))]
    *moved, side = tie(*moved, side)
    attention, normed = middle(picked, own, moved, gain2[None, :])

    moved = [cross(normed, d, True) for d in (1, 2, 3)]
    others = [swap(merged), swap(near), swap(side)]
    *moved, others[0], others[1], others[2] = tie(*moved, *others)
    row = join([normed] + moved)
    xs = [row] + [cross(row, e, False) for e in (1, 2, 3)]
    *xs, far = tie(*xs, far)
    outs = feed(place, xs, [merged, near, side, far] + others + [swap(far)])
    own, s1, s2, s3 = fold([outs[0]] + [cross(outs[e], 4 - e, False) for e in (1, 2, 3)])
    outs = [own] + [cross(s, 4 - d, True) for d, s in ((1, s1), (2, s2), (3, s3))]

    mine = lax.dynamic_slice_in_dim(chosen, own_at, OWN, 0)
    hit = mine[:, None] == jnp.arange(SEQ_DEV, dtype=jnp.int32)[None, :]
    router = jax.nn.sigmoid(jnp.sum(jnp.where(hit, preference[None, :], 0.0), axis=1, keepdims=True))
    result = finish(picked, attention, router, outs)
    rows = join([result] + [shift(result, "x", d) for d in (1, 2, 3)])
    return put_back(info, chosen[None, :], block, [rows, swap(rows)])


def solution(mesh):
    grid = Mesh(mesh.devices.reshape(4, 4, 4, 2), ("y", "z", "x", "c"))
    ctx, mp = ("y", "z"), ("x", "c")
    return jax.shard_map(
        local,
        mesh=grid,
        in_specs=(P(ctx, None), P(ctx), P(ctx), P(ctx), P(), P(None, mp), P(None, mp), P(None, mp),
                  P(mp, None), P(mp), P(), P(ctx, mp), P(ctx, mp), P(ctx, mp)),
        out_specs=P(ctx, None),
        check_vma=False,
    )
```

```python
import functools
import math

import jax
import jax.numpy as jnp
from jax import lax
from jax.experimental import pallas as pl
from jax.experimental.pallas import tpu as pltpu
from jax.sharding import Mesh, PartitionSpec as P
import numpy as np

D = 2304
CAP = 256
SEQ_DEV = 1024
HD = 128
FF_DEV = 1152
ROWS = 144
STEP = 512
OWN = 32
EPS = 1e-06
NEG = -1e30
LOG2E = 1.4426950408889634
MB = 1024 * 1024
F32 = jnp.float32
BF16 = jnp.bfloat16


def vmem_spec():
    return pl.BlockSpec(memory_space=pltpu.VMEM)


def smem_spec():
    return pl.BlockSpec(memory_space=pltpu.SMEM)


def hbm_spec():
    return pl.BlockSpec(memory_space=pltpu.HBM)


def params(mib):
    return pltpu.CompilerParams(vmem_limit_bytes=mib * MB)


def begin_body(occupied, block_hbm, chosen, gain, frequency, wq_hbm, wk_hbm, wv_hbm,
               q_out, kv_out, own_out, block, picked, normed, wq, wk, wv, sems):
    tiles = D // 256
    loads = [pltpu.make_async_copy(block_hbm.at[:, i * 256:(i + 1) * 256],
                                   block.at[:, i * 256:(i + 1) * 256], sems.at[i])
             for i in range(tiles)]
    weights = [pltpu.make_async_copy(src, dst, sems.at[9 + i])
               for i, (src, dst) in enumerate(((wk_hbm, wk), (wv_hbm, wv), (wq_hbm, wq)))]
    for copy in loads + weights:
        copy.start()
    wide = jnp.broadcast_to(chosen[...].astype(F32), (128, CAP))
    column = jnp.transpose(wide)[:, 0:1].astype(jnp.int32)
    shard = 4 * lax.axis_index("y") + lax.axis_index("z")
    angles = (column + shard * SEQ_DEV).astype(F32) * frequency[...]
    cosine, sine = jnp.cos(angles), jnp.sin(angles)
    sine = jnp.where(lax.broadcasted_iota(jnp.int32, (CAP, HD), 1) < HD // 2, -sine, sine)
    lanes = lax.broadcasted_iota(jnp.int32, (CAP, SEQ_DEV), 1)
    one_hot = jnp.where(lanes == column, 1.0, 0.0).astype(BF16)
    total = jnp.zeros((CAP, 256), F32)
    for i in range(tiles):
        cols = slice(i * 256, (i + 1) * 256)
        loads[i].wait()
        part = jnp.dot(one_hot, block[:, cols], preferred_element_type=F32)
        picked[:, cols] = part.astype(BF16)
        total = total + part * part
    inv = lax.rsqrt(jnp.sum(total, axis=1, keepdims=True) / D + EPS)
    for i in range(tiles):
        cols = slice(i * 256, (i + 1) * 256)
        normed[:, cols] = (picked[:, cols].astype(F32) * inv * gain[:, cols]).astype(BF16)
    first = lax.axis_index("c") * 128 + lax.axis_index("x") * OWN
    own_out[...] = picked[pl.ds(pl.multiple_of(first, OWN), OWN), :]

    def turn(values):
        return values * cosine + pltpu.roll(values, HD // 2, 1) * sine

    weights[0].wait()
    keys = jnp.dot(normed[...], wk[...], preferred_element_type=F32)
    for h in range(2):
        kv_out[h * HD:(h + 1) * HD, 0:CAP] = jnp.transpose(turn(keys[:, h * HD:(h + 1) * HD])).astype(BF16)
    weights[1].wait()
    kv_out[0:CAP, 256:512] = jnp.dot(normed[...], wv[...], preferred_element_type=F32).astype(BF16)
    kv_out[CAP:CAP + 16, :] = jnp.full((16, 512), occupied[0].astype(F32), F32).astype(BF16)
    weights[2].wait()
    for j in range(2):
        part = jnp.dot(normed[...], wq[:, j * 256:(j + 1) * 256], preferred_element_type=F32)
        for h in range(2):
            at = j * 256 + h * HD
            q_out[:, at:at + HD] = turn(part[:, h * HD:(h + 1) * HD]).astype(BF16)


def begin(occupied, block, chosen, gain, frequency, wq, wk, wv):
    return pl.pallas_call(
        begin_body,
        out_shape=(jax.ShapeDtypeStruct((CAP, 512), BF16), jax.ShapeDtypeStruct((CAP + 16, 512), BF16),
                   jax.ShapeDtypeStruct((OWN, D), BF16)),
        in_specs=[smem_spec(), hbm_spec()] + [vmem_spec()] * 3 + [hbm_spec()] * 3,
        out_specs=(vmem_spec(),) * 3,
        scratch_shapes=[pltpu.VMEM((SEQ_DEV, D), BF16), pltpu.VMEM((CAP, D), BF16), pltpu.VMEM((CAP, D), BF16),
                        pltpu.VMEM((D, 512), BF16), pltpu.VMEM((D, 256), BF16), pltpu.VMEM((D, 256), BF16),
                        pltpu.SemaphoreType.DMA((12,))],
        compiler_params=params(60),
        name="begin",
    )(occupied, block, chosen, gain, frequency, wq, wk, wv)


def pack_body(gate, up, down, out0, out1, packed, sems):
    loads, stores = [], []
    for s, out in enumerate((out0, out1)):
        cols = pl.ds(pl.multiple_of(lax.rem(lax.axis_index("y") + s, 2) * FF_DEV, FF_DEV), FF_DEV)
        for k, weight in enumerate((gate, up, down)):
            rows = slice(k * ROWS, (k + 1) * ROWS)
            at = 3 * s + k
            loads.append(pltpu.make_async_copy(weight.at[:, cols], packed.at[s, rows, :], sems.at[at]))
            stores.append(pltpu.make_async_copy(packed.at[s, rows, :], out.at[rows, :], sems.at[6 + at]))
    for load in loads:
        load.start()
    for load, store in zip(loads, stores):
        load.wait()
        store.start()
    for store in stores:
        store.wait()


def pack(gate, up, down):
    return pl.pallas_call(
        pack_body,
        out_shape=(jax.ShapeDtypeStruct((3 * ROWS, FF_DEV), BF16),) * 2,
        in_specs=[hbm_spec()] * 3,
        out_specs=(hbm_spec(),) * 2,
        scratch_shapes=[pltpu.VMEM((2, 3 * ROWS, FF_DEV), BF16), pltpu.SemaphoreType.DMA((12,))],
        compiler_params=params(60),
        name="pack",
    )(gate, up, down)


def attend_body(diagonal, at, scale, q, kv0, kv1, kv2, kv3, out, stats):
    lane = lax.broadcasted_iota(jnp.int32, (1, CAP), 1).astype(F32)
    bias = []
    kvs = (kv0, kv1, kv2, kv3)
    for j, kv in enumerate(kvs):
        count = kv[CAP:CAP + 16, 0:CAP].astype(F32)[0:1, :]
        live = (lane < count) & (at[j] >= 0)
        bias.append(jnp.where(live, 0.0, NEG))
    past = lax.broadcasted_iota(jnp.int32, (CAP, CAP), 1) - lax.broadcasted_iota(jnp.int32, (CAP, CAP), 0)
    for head in range(4):
        g = head // 2
        cols = slice(head * HD, (head + 1) * HD)
        query = q[:, cols]
        scores = []
        for j in range(4):
            part = jnp.dot(query, kvs[j][g * HD:(g + 1) * HD, 0:CAP], preferred_element_type=F32)
            part = part * scale[head] + bias[j]
            if diagonal:
                part = jnp.where(past <= at[j], part, NEG)
            scores.append(part)
        top = jnp.max(functools.reduce(jnp.maximum, scores), axis=1, keepdims=True)
        weights = [jnp.exp2(part - top) for part in scores]
        total = jnp.sum(functools.reduce(jnp.add, weights), axis=1, keepdims=True)
        mixed = jnp.zeros((CAP, HD), F32)
        for j, kv in enumerate(kvs):
            mixed = mixed + jnp.dot(weights[j].astype(BF16), kv[0:CAP, 256 + g * HD:256 + (g + 1) * HD],
                                    preferred_element_type=F32)
        out[0:CAP, cols] = (mixed * (1.0 / total)).astype(BF16)
        log_sum = top + jnp.log2(total)
        first = log_sum.astype(BF16).astype(F32)
        second = (log_sum - first).astype(BF16).astype(F32)
        stats[:, head:head + 1] = first
        stats[:, 4 + head:5 + head] = second
        stats[:, 8 + head:9 + head] = log_sum - first - second
    lanes = lax.broadcasted_iota(jnp.int32, (CAP, 128), 1)
    clean = jnp.where(lanes < 12, stats[...], 0.0)
    out[CAP:CAP + 16, 0:CAP] = jnp.transpose(clean)[0:16, :].astype(BF16)
    out[CAP:CAP + 16, CAP:512] = jnp.zeros((16, 512 - CAP), BF16)


def attend(diagonal, at, scale, q, kvs):
    return pl.pallas_call(
        functools.partial(attend_body, diagonal),
        out_shape=jax.ShapeDtypeStruct((CAP + 16, 512), BF16),
        in_specs=[smem_spec()] * 2 + [vmem_spec()] * 5,
        out_specs=vmem_spec(),
        scratch_shapes=[pltpu.VMEM((CAP, 128), F32)],
        compiler_params=params(12),
        name="attend",
    )(at, scale, q, *kvs)


def mix_body(p0, p1, p2, p3, wo_hbm, keep, send, mixed, wo, sem):
    load = pltpu.make_async_copy(wo_hbm, wo, sem)
    load.start()
    parts = (p0, p1, p2, p3)
    logs = []
    for part in parts:
        rows = part[CAP:CAP + 16, 0:CAP].astype(F32)
        rows = jnp.concatenate([rows, jnp.zeros((112, CAP), F32)], axis=0)
        logs.append(jnp.transpose(rows))
    for head in range(4):
        cols = slice(head * HD, (head + 1) * HD)
        each = [log[:, head:head + 1] + log[:, 4 + head:5 + head] + log[:, 8 + head:9 + head] for log in logs]
        top = functools.reduce(jnp.maximum, each)
        weights = [jnp.exp2(one - top) for one in each]
        total = functools.reduce(jnp.add, weights)
        value = functools.reduce(jnp.add, [w * part[0:CAP, cols].astype(F32) for w, part in zip(weights, parts)])
        mixed[:, cols] = (value / total).astype(BF16)
    core = lax.axis_index("c")
    mine = mixed[pl.ds(pl.multiple_of(core * 128, 128), 128), :]
    other = mixed[pl.ds(pl.multiple_of((1 - core) * 128, 128), 128), :]

    load.wait()
    for i in range(D // 256):
        cols = slice(i * 256, (i + 1) * 256)
        send[:, cols] = jnp.dot(other, wo[:, cols], preferred_element_type=F32).astype(BF16)
        keep[:, cols] = jnp.dot(mine, wo[:, cols], preferred_element_type=F32)


def mix(parts, wo):
    return pl.pallas_call(
        mix_body,
        out_shape=(jax.ShapeDtypeStruct((128, D), F32), jax.ShapeDtypeStruct((128, D), BF16)),
        in_specs=[vmem_spec()] * 4 + [hbm_spec()],
        out_specs=(vmem_spec(),) * 2,
        scratch_shapes=[pltpu.VMEM((CAP, 512), BF16), pltpu.VMEM((512, D), BF16), pltpu.SemaphoreType.DMA],
        compiler_params=params(16),
        name="mix",
    )(*parts, wo)


def split_body(keep, got, own, s1, s2, s3):
    x = lax.axis_index("x")
    for d, ref in enumerate((own, s1, s2, s3)):
        rows = pl.ds(pl.multiple_of(lax.rem(x + d, 4) * OWN, OWN), OWN)
        ref[...] = (keep[rows, :] + got[rows, :].astype(F32)).astype(ref.dtype)


def split(keep, got):
    piece = jax.ShapeDtypeStruct((OWN, D), BF16)
    return pl.pallas_call(
        split_body,
        out_shape=(jax.ShapeDtypeStruct((OWN, D), F32), piece, piece, piece),
        in_specs=[vmem_spec()] * 2,
        out_specs=(vmem_spec(),) * 4,
        compiler_params=params(12),
        name="split",
    )(keep, got)


def middle_body(picked, own, r1, r2, r3, gain, attention, normed):
    total = own[...] + r1[...].astype(F32) + r2[...].astype(F32) + r3[...].astype(F32)
    attention[...] = total
    mid = (picked[...].astype(F32) + total).astype(BF16).astype(F32)
    inv = lax.rsqrt(jnp.mean(mid * mid, axis=1, keepdims=True) + EPS)
    normed[...] = (mid * inv * gain[...]).astype(BF16)


def middle(picked, own, got, gain):
    return pl.pallas_call(
        middle_body,
        out_shape=(jax.ShapeDtypeStruct((OWN, D), F32), jax.ShapeDtypeStruct((OWN, D), BF16)),
        in_specs=[vmem_spec()] * 6,
        out_specs=(vmem_spec(),) * 2,
        compiler_params=params(12),
        name="middle",
    )(picked, own, *got, gain)


def feed_body(*refs):
    place = refs[0]
    xs = refs[1:5]
    pieces = refs[5:13]
    outs = refs[13:17]
    tokens, gate, up, down, hidden, sems = refs[17:]
    copies = [[], [], []]
    for e, x in enumerate(xs):
        copies[0].append(pltpu.make_async_copy(x, tokens.at[e * 128:(e + 1) * 128, :], sems.at[e]))
    for k, weight in enumerate((gate, up, down)):
        for i in range(16):
            rows = pl.ds(pl.multiple_of(place[i] * ROWS, 16), ROWS)
            at = (3 * (i % 2) + k) * ROWS
            copies[k].append(pltpu.make_async_copy(pieces[i // 2].at[at:at + ROWS, :], weight.at[rows, :],
                                                   sems.at[4 + 16 * k + i]))
    for copy in copies[0] + copies[1] + copies[2]:
        copy.start()
    for copy in copies[0]:
        copy.wait()
    chunks = [slice(j * 256, min((j + 1) * 256, FF_DEV)) for j in range(5)]
    for j, cols in enumerate(chunks):
        one = jnp.dot(tokens[...], gate[:, cols], preferred_element_type=F32)
        if j == 0:
            for copy in copies[1]:
                copy.wait()
        two = jnp.dot(tokens[...], up[:, cols], preferred_element_type=F32)
        hidden[:, cols] = (one / (1.0 + jnp.exp(-one)) * two).astype(BF16)
    for copy in copies[2]:
        copy.wait()
    for n in range(D // 256):
        rows = slice(n * 256, (n + 1) * 256)
        part = lax.dot_general(hidden[...], down[rows, :], (((1,), (1,)), ((), ())),
                               preferred_element_type=F32).astype(BF16)
        for e, out in enumerate(outs):
            out[:, rows] = part[e * 128:(e + 1) * 128, :]


def feed(place, xs, pieces):
    return pl.pallas_call(
        feed_body,
        out_shape=(jax.ShapeDtypeStruct((4 * OWN, D), BF16),) * 4,
        in_specs=[smem_spec()] + [hbm_spec()] * 12,
        out_specs=(vmem_spec(),) * 4,
        scratch_shapes=[pltpu.VMEM((512, D), BF16), pltpu.VMEM((D, FF_DEV), BF16), pltpu.VMEM((D, FF_DEV), BF16),
                        pltpu.VMEM((D, FF_DEV), BF16), pltpu.VMEM((512, FF_DEV), BF16),
                        pltpu.SemaphoreType.DMA((52,))],
        compiler_params=params(60),
        name="feed",
    )(place, *xs, *pieces)


def fold_body(p0, p1, p2, p3, own, s1, s2, s3):
    for d, out in enumerate((own, s1, s2, s3)):
        rows = slice(d * OWN, (d + 1) * OWN)
        total = p0[rows, :].astype(F32) + p1[rows, :].astype(F32)
        out[...] = (total + p2[rows, :].astype(F32) + p3[rows, :].astype(F32)).astype(out.dtype)


def fold(parts):
    piece = jax.ShapeDtypeStruct((OWN, D), BF16)
    return pl.pallas_call(
        fold_body,
        out_shape=(jax.ShapeDtypeStruct((OWN, D), F32), piece, piece, piece),
        in_specs=[vmem_spec()] * 4,
        out_specs=(vmem_spec(),) * 4,
        compiler_params=params(12),
        name="fold",
    )(*parts)


def finish_body(picked, attention, gate, own, r1, r2, r3, out):
    total = attention[...] + own[...]
    total = total + r1[...].astype(F32) + r2[...].astype(F32) + r3[...].astype(F32)
    out[...] = (picked[...].astype(F32) + gate[...] * total).astype(BF16)


def finish(picked, attention, gate, parts):
    return pl.pallas_call(
        finish_body,
        out_shape=jax.ShapeDtypeStruct((OWN, D), BF16),
        in_specs=[vmem_spec()] * 7,
        out_specs=vmem_spec(),
        compiler_params=params(12),
        name="finish",
    )(picked, attention, gate, *parts)


def merge_body(first, second, out, sems):
    copies = [pltpu.make_async_copy(ref, out.at[s * 3 * ROWS:(s + 1) * 3 * ROWS, :], sems.at[s])
              for s, ref in enumerate((first, second))]
    for copy in copies:
        copy.start()
    for copy in copies:
        copy.wait()


def merge(first, second):
    return pl.pallas_call(
        merge_body,
        out_shape=jax.ShapeDtypeStruct((6 * ROWS, FF_DEV), BF16),
        in_specs=[hbm_spec()] * 2,
        out_specs=vmem_spec(),
        scratch_shapes=[pltpu.SemaphoreType.DMA((2,))],
        compiler_params=params(60),
        name="merge",
    )(first, second)


def join_body(*refs):
    for i, ref in enumerate(refs[:4]):
        refs[4][i * OWN:(i + 1) * OWN, :] = ref[...]


def join(pieces):
    return pl.pallas_call(
        join_body,
        out_shape=jax.ShapeDtypeStruct((4 * OWN, D), BF16),
        in_specs=[vmem_spec()] * 4,
        out_specs=vmem_spec(),
        compiler_params=params(12),
        name="join",
    )(*pieces)


def hold_body(block, out, sem):
    copy = pltpu.make_async_copy(block, out, sem)
    copy.start()
    copy.wait()


def hold(block):
    return pl.pallas_call(
        hold_body,
        out_shape=jax.ShapeDtypeStruct((SEQ_DEV, D), BF16),
        in_specs=[hbm_spec()],
        out_specs=vmem_spec(),
        scratch_shapes=[pltpu.SemaphoreType.DMA],
        compiler_params=params(20),
        name="hold",
    )(block)


def place_body(occupied, chosen, block, *refs):
    pieces = refs[:2]
    out = refs[2]
    rows = refs[3]

    @pl.when(pl.program_id(0) == 0)
    def _():
        for core, piece in enumerate(pieces):
            for dx in range(4):
                at = lax.rem(lax.axis_index("c") + core, 2) * 128 + lax.rem(lax.axis_index("x") + 4 - dx, 4) * OWN
                rows[pl.ds(pl.multiple_of(at, OWN), OWN), :] = piece[dx * OWN:(dx + 1) * OWN, :]

    position = lax.broadcasted_iota(jnp.int32, (STEP, CAP), 0) + pl.program_id(0) * STEP
    slot = lax.broadcasted_iota(jnp.int32, (STEP, CAP), 1)
    hit = jnp.where((position == chosen[...]) & (slot < occupied[0]), 1.0, 0.0)
    taken = jnp.sum(hit, axis=1, keepdims=True) > 0.5
    hit = hit.astype(BF16)
    for n in range(D // 256):
        cols = slice(n * 256, (n + 1) * 256)
        new = jnp.dot(hit, rows[:, cols], preferred_element_type=F32).astype(BF16)
        out[:, cols] = jnp.where(taken, new, block[:, cols])


def put_back(occupied, chosen, block, pieces):
    return pl.pallas_call(
        place_body,
        grid=(SEQ_DEV // STEP,),
        out_shape=jax.ShapeDtypeStruct((SEQ_DEV, D), BF16),
        in_specs=[smem_spec(), pl.BlockSpec((1, CAP), lambda i: (0, 0)),
                  pl.BlockSpec((STEP, D), lambda i: (i, 0))]
        + [pl.BlockSpec((128, D), lambda i: (0, 0))] * 2,
        out_specs=pl.BlockSpec((STEP, D), lambda i: (i, 0)),
        scratch_shapes=[pltpu.VMEM((CAP, D), BF16)],
        compiler_params=params(20),
        name="put_back",
    )(occupied, chosen, block, *pieces)


def shift(value, axis, step, size=4):
    return lax.ppermute(value, axis, [(i, (i + step) % size) for i in range(size)])


def cross(value, step, first):
    pairs = []
    for y in range(4):
        for x in range(4):
            for c in range(2):
                along_x = (c == 0) == first
                to_y, to_x = (y, (x + step) % 4) if along_x else ((y + step) % 4, x)
                pairs.append((8 * y + 2 * x + c, 8 * to_y + 2 * to_x + c))
    return lax.ppermute(value, ("y", "x", "c"), pairs)


def around(value, step):
    pairs = [(2 * z + c, 2 * ((z + (step if c == 0 else 4 - step)) % 4) + c) for z in range(4) for c in range(2)]
    return lax.ppermute(value, ("z", "c"), pairs)


def swap(value):
    return shift(value, "c", 1, 2)


def weight_pairs(s):
    return [(2 * sy + sc, 2 * (2 * sc + (sy + s) % 2) + sy // 2) for sy in range(4) for sc in range(2)]


def tie(*values):
    return lax.optimization_barrier(values)


def local(block, preference, chosen, occupied, gain1, wq, wk, wv, wo, sharpness, gain2, gate_w, up_w, down_w):
    y, z, x, c = (lax.axis_index(n) for n in ("y", "z", "x", "c"))
    own_at = c * 128 + x * OWN
    near = 3 - 2 * c
    place = []
    for core, step in ((c, near), (1 - c, 4 - near)):
        for source in (z, z + step, z + 4 - step, z + 2):
            for s in range(2):
                place.append(4 * (2 * core + (y + s) % 2) + source % 4)
    place = jnp.stack(place).astype(jnp.int32)

    frequency = 10000.0 ** (-(np.arange(HD) % (HD // 2)) / (HD // 2))
    frequency = jnp.asarray(frequency.astype(np.float32)[None, :])
    packs = pack(gate_w, up_w, down_w)
    *packs, occupied = tie(*packs, occupied)
    got = [lax.ppermute(p, ("y", "c"), weight_pairs(s)) for s, p in enumerate(packs)]
    q, kv, picked = begin(occupied, block, chosen[None, :], gain1[None, :], frequency, wq, wk, wv)

    kvs = [kv] + [shift(kv, "z", d) for d in (1, 2, 3)]
    q, *got = tie(q, *got)
    asked = [shift(q, "y", d) for d in (1, 2, 3)]
    merged = merge(*got)

    scale = sharpness * (LOG2E / math.sqrt(HD))
    at = jnp.stack([z * 0] + [jnp.where(z >= d, CAP, -CAP) for d in (1, 2, 3)]).astype(jnp.int32)
    mine = attend(True, at, scale, q, kvs)
    mine, merged = tie(mine, merged)
    near, side = around(merged, 1), around(merged, 3)
    asked[0], mine = tie(asked[0], mine)
    parts = [mine]
    for d in (1, 2, 3):
        at = jnp.broadcast_to(jnp.where((y - d) % 4 > y, CAP, -CAP), (4,)).astype(jnp.int32)
        parts.append(shift(attend(False, at, scale, asked[d - 1], kvs), "y", 4 - d))

    keep, send = mix(parts, wo)
    own, s1, s2, s3 = split(keep, swap(send))
    moved = [shift(s, "x", d) for d, s in ((1, s1), (2, s2), (3, s3))]
    *moved, near, side = tie(*moved, near, side)
    far = around(near, 1)
    attention, normed = middle(picked, own, moved, gain2[None, :])

    moved = [cross(normed, d, True) for d in (1, 2, 3)]
    others = [swap(piece) for piece in (merged, near, side)]
    *moved, others[0], others[1] = tie(*moved, *others[:2])
    row = join([normed] + moved)
    xs = [row] + [cross(row, e, False) for e in (1, 2, 3)]
    *xs, others[2], far = tie(*xs, others[2], far)
    others.append(swap(far))
    outs = feed(place, xs, [merged, near, side, far] + others)
    own, s1, s2, s3 = fold([outs[0]] + [cross(outs[e], 4 - e, False) for e in (1, 2, 3)])
    outs = [own] + [cross(s, 4 - d, True) for d, s in ((1, s1), (2, s2), (3, s3))]

    mine = lax.dynamic_slice_in_dim(chosen, own_at, OWN, 0)
    hit = mine[:, None] == jnp.arange(SEQ_DEV, dtype=jnp.int32)[None, :]
    router = jax.nn.sigmoid(jnp.sum(jnp.where(hit, preference[None, :], 0.0), axis=1, keepdims=True))
    result = finish(picked, attention, router, outs)
    *rows, block = tie(*[shift(result, "x", d) for d in (1, 2, 3)], hold(block))
    rows = join([result] + rows)
    return put_back(occupied, chosen[None, :], block, [rows, swap(rows)])


def solution(mesh):
    grid = Mesh(mesh.devices.reshape(4, 4, 4, 2), ("y", "z", "x", "c"))
    ctx, mp = ("y", "z"), ("x", "c")
    return jax.shard_map(
        local,
        mesh=grid,
        in_specs=(P(ctx, None), P(ctx), P(ctx), P(ctx), P(), P(None, mp), P(None, mp), P(None, mp),
                  P(mp, None), P(mp), P(), P(ctx, mp), P(ctx, mp), P(ctx, mp)),
        out_specs=P(ctx, None),
        check_vma=False,
    )
```

```python
import functools
import math

import jax
import jax.numpy as jnp
from jax import lax
from jax.experimental import pallas as pl
from jax.experimental.pallas import tpu as pltpu
from jax.sharding import Mesh, PartitionSpec as P
import numpy as np

D = 2304
CAP = 256
SEQ_DEV = 1024
HD = 128
FF_DEV = 1152
ROWS = 144
STEP = 512
OWN = 32
EPS = 1e-06
NEG = -1e30
LOG2E = 1.4426950408889634
MB = 1024 * 1024
F32 = jnp.float32
BF16 = jnp.bfloat16


def vmem_spec():
    return pl.BlockSpec(memory_space=pltpu.VMEM)


def smem_spec():
    return pl.BlockSpec(memory_space=pltpu.SMEM)


def hbm_spec():
    return pl.BlockSpec(memory_space=pltpu.HBM)


def params(mib):
    return pltpu.CompilerParams(vmem_limit_bytes=mib * MB)


def begin_body(occupied, block_hbm, chosen, gain, frequency, wq_hbm, wk_hbm, wv_hbm,
               q_out, kv_hbm, own_out, block, picked, normed, wq, wk, wv, kv_out, sems):
    tiles = D // 256
    loads = [pltpu.make_async_copy(block_hbm.at[:, i * 256:(i + 1) * 256],
                                   block.at[:, i * 256:(i + 1) * 256], sems.at[i])
             for i in range(tiles)]
    weights = [pltpu.make_async_copy(src, dst, sems.at[9 + i])
               for i, (src, dst) in enumerate(((wk_hbm, wk), (wv_hbm, wv), (wq_hbm, wq)))]
    for copy in loads:
        copy.start()
    wide = jnp.broadcast_to(chosen[...].astype(F32), (128, CAP))
    column = jnp.transpose(wide)[:, 0:1].astype(jnp.int32)
    shard = 4 * lax.axis_index("y") + lax.axis_index("z")
    angles = (column + shard * SEQ_DEV).astype(F32) * frequency[...]
    cosine, sine = jnp.cos(angles), jnp.sin(angles)
    sine = jnp.where(lax.broadcasted_iota(jnp.int32, (CAP, HD), 1) < HD // 2, -sine, sine)
    lanes = lax.broadcasted_iota(jnp.int32, (CAP, SEQ_DEV), 1)
    one_hot = jnp.where(lanes == column, 1.0, 0.0).astype(BF16)
    total = jnp.zeros((CAP, 256), F32)
    for i in range(tiles):
        cols = slice(i * 256, (i + 1) * 256)
        loads[i].wait()
        if i == 4:
            for copy in weights:
                copy.start()
        part = jnp.dot(one_hot, block[:, cols], preferred_element_type=F32)
        picked[:, cols] = part.astype(BF16)
        total = total + part * part
    inv = lax.rsqrt(jnp.sum(total, axis=1, keepdims=True) / D + EPS)
    for i in range(tiles):
        cols = slice(i * 256, (i + 1) * 256)
        normed[:, cols] = (picked[:, cols].astype(F32) * inv * gain[:, cols]).astype(BF16)
    first = lax.axis_index("c") * 128 + lax.axis_index("x") * OWN
    own_out[...] = picked[pl.ds(pl.multiple_of(first, OWN), OWN), :]

    def turn(values):
        return values * cosine + pltpu.roll(values, HD // 2, 1) * sine

    weights[0].wait()
    keys = jnp.dot(normed[...], wk[...], preferred_element_type=F32)
    for h in range(2):
        kv_out[h * HD:(h + 1) * HD, 0:CAP] = jnp.transpose(turn(keys[:, h * HD:(h + 1) * HD])).astype(BF16)
    weights[1].wait()
    kv_out[0:CAP, 256:512] = jnp.dot(normed[...], wv[...], preferred_element_type=F32).astype(BF16)
    kv_out[CAP:CAP + 16, :] = jnp.full((16, 512), occupied[0].astype(F32), F32).astype(BF16)
    stores = [pltpu.make_async_copy(kv_out, kv_hbm.at[n], sems.at[n]) for n in range(4)]
    for copy in stores:
        copy.start()
    weights[2].wait()
    for j in range(2):
        part = jnp.dot(normed[...], wq[:, j * 256:(j + 1) * 256], preferred_element_type=F32)
        for h in range(2):
            at = j * 256 + h * HD
            q_out[:, at:at + HD] = turn(part[:, h * HD:(h + 1) * HD]).astype(BF16)
    for copy in stores:
        copy.wait()


def begin(occupied, block, chosen, gain, frequency, wq, wk, wv):
    return pl.pallas_call(
        begin_body,
        out_shape=(jax.ShapeDtypeStruct((CAP, 512), BF16), jax.ShapeDtypeStruct((4, CAP + 16, 512), BF16),
                   jax.ShapeDtypeStruct((OWN, D), BF16)),
        in_specs=[smem_spec(), hbm_spec()] + [vmem_spec()] * 3 + [hbm_spec()] * 3,
        out_specs=(vmem_spec(), hbm_spec(), vmem_spec()),
        scratch_shapes=[pltpu.VMEM((SEQ_DEV, D), BF16), pltpu.VMEM((CAP, D), BF16), pltpu.VMEM((CAP, D), BF16),
                        pltpu.VMEM((D, 512), BF16), pltpu.VMEM((D, 256), BF16), pltpu.VMEM((D, 256), BF16),
                        pltpu.VMEM((CAP + 16, 512), BF16),
                        pltpu.SemaphoreType.DMA((12,))],
        compiler_params=params(60),
        name="begin",
    )(occupied, block, chosen, gain, frequency, wq, wk, wv)


def pack_body(gate, up, down, out0, out1, packed, sems):
    loads, stores = [], []
    for s, out in enumerate((out0, out1)):
        cols = pl.ds(pl.multiple_of(lax.rem(lax.axis_index("y") + s, 2) * FF_DEV, FF_DEV), FF_DEV)
        for k, weight in enumerate((gate, up, down)):
            rows = slice(k * ROWS, (k + 1) * ROWS)
            at = 3 * s + k
            loads.append(pltpu.make_async_copy(weight.at[:, cols], packed.at[s, rows, :], sems.at[at]))
            stores.append(pltpu.make_async_copy(packed.at[s, rows, :], out.at[rows, :], sems.at[6 + at]))
    for load in loads:
        load.start()
    for load, store in zip(loads, stores):
        load.wait()
        store.start()
    for store in stores:
        store.wait()


def pack(gate, up, down):
    return pl.pallas_call(
        pack_body,
        out_shape=(jax.ShapeDtypeStruct((3 * ROWS, FF_DEV), BF16),) * 2,
        in_specs=[hbm_spec()] * 3,
        out_specs=(hbm_spec(),) * 2,
        scratch_shapes=[pltpu.VMEM((2, 3 * ROWS, FF_DEV), BF16), pltpu.SemaphoreType.DMA((12,))],
        compiler_params=params(60),
        name="pack",
    )(gate, up, down)


def attend_body(diagonal, at, scale, q, kv, out, stats):
    lane = lax.broadcasted_iota(jnp.int32, (1, CAP), 1).astype(F32)
    bias = []
    for j in range(4):
        count = kv[j, CAP:CAP + 16, 0:CAP].astype(F32)[0:1, :]
        live = (lane < count) & (at[j] >= 0)
        bias.append(jnp.where(live, 0.0, NEG))
    past = lax.broadcasted_iota(jnp.int32, (CAP, CAP), 1) - lax.broadcasted_iota(jnp.int32, (CAP, CAP), 0)
    for head in range(4):
        g = head // 2
        cols = slice(head * HD, (head + 1) * HD)
        query = q[:, cols]
        scores = []
        for j in range(4):
            part = jnp.dot(query, kv[j, g * HD:(g + 1) * HD, 0:CAP], preferred_element_type=F32)
            part = part * scale[head] + bias[j]
            if diagonal:
                part = jnp.where(past <= at[j], part, NEG)
            scores.append(part)
        top = jnp.max(functools.reduce(jnp.maximum, scores), axis=1, keepdims=True)
        weights = [jnp.exp2(part - top) for part in scores]
        total = jnp.sum(functools.reduce(jnp.add, weights), axis=1, keepdims=True)
        mixed = jnp.zeros((CAP, HD), F32)
        for j in range(4):
            mixed = mixed + jnp.dot(weights[j].astype(BF16), kv[j, 0:CAP, 256 + g * HD:256 + (g + 1) * HD],
                                    preferred_element_type=F32)
        out[0:CAP, cols] = (mixed * (1.0 / total)).astype(BF16)
        log_sum = top + jnp.log2(total)
        first = log_sum.astype(BF16).astype(F32)
        second = (log_sum - first).astype(BF16).astype(F32)
        stats[:, head:head + 1] = first
        stats[:, 4 + head:5 + head] = second
        stats[:, 8 + head:9 + head] = log_sum - first - second
    lanes = lax.broadcasted_iota(jnp.int32, (CAP, 128), 1)
    clean = jnp.where(lanes < 12, stats[...], 0.0)
    out[CAP:CAP + 16, 0:CAP] = jnp.transpose(clean)[0:16, :].astype(BF16)
    out[CAP:CAP + 16, CAP:512] = jnp.zeros((16, 512 - CAP), BF16)


def attend(diagonal, at, scale, q, kv):
    return pl.pallas_call(
        functools.partial(attend_body, diagonal),
        out_shape=jax.ShapeDtypeStruct((CAP + 16, 512), BF16),
        in_specs=[smem_spec()] * 2 + [vmem_spec()] * 2,
        out_specs=vmem_spec(),
        scratch_shapes=[pltpu.VMEM((CAP, 128), F32)],
        compiler_params=params(12),
        name="attend",
    )(at, scale, q, kv)


def mix_body(p0, p1, p2, p3, wo_hbm, keep, send, mixed, wo, sem):
    load = pltpu.make_async_copy(wo_hbm, wo, sem)
    load.start()
    parts = (p0, p1, p2, p3)
    logs = []
    for part in parts:
        rows = part[CAP:CAP + 16, 0:CAP].astype(F32)
        rows = jnp.concatenate([rows, jnp.zeros((112, CAP), F32)], axis=0)
        logs.append(jnp.transpose(rows))
    for head in range(4):
        cols = slice(head * HD, (head + 1) * HD)
        each = [log[:, head:head + 1] + log[:, 4 + head:5 + head] + log[:, 8 + head:9 + head] for log in logs]
        top = functools.reduce(jnp.maximum, each)
        weights = [jnp.exp2(one - top) for one in each]
        total = functools.reduce(jnp.add, weights)
        value = functools.reduce(jnp.add, [w * part[0:CAP, cols].astype(F32) for w, part in zip(weights, parts)])
        mixed[:, cols] = (value / total).astype(BF16)
    core = lax.axis_index("c")
    mine = mixed[pl.ds(pl.multiple_of(core * 128, 128), 128), :]
    other = mixed[pl.ds(pl.multiple_of((1 - core) * 128, 128), 128), :]

    load.wait()
    for i in range(D // 256):
        cols = slice(i * 256, (i + 1) * 256)
        send[:, cols] = jnp.dot(other, wo[:, cols], preferred_element_type=F32).astype(BF16)
        keep[:, cols] = jnp.dot(mine, wo[:, cols], preferred_element_type=F32)


def mix(parts, wo):
    return pl.pallas_call(
        mix_body,
        out_shape=(jax.ShapeDtypeStruct((128, D), F32), jax.ShapeDtypeStruct((128, D), BF16)),
        in_specs=[vmem_spec()] * 4 + [hbm_spec()],
        out_specs=(vmem_spec(),) * 2,
        scratch_shapes=[pltpu.VMEM((CAP, 512), BF16), pltpu.VMEM((512, D), BF16), pltpu.SemaphoreType.DMA],
        compiler_params=params(16),
        name="mix",
    )(*parts, wo)


def split_body(keep, got, own, s1, s2, s3):
    x = lax.axis_index("x")
    for d, ref in enumerate((own, s1, s2, s3)):
        rows = pl.ds(pl.multiple_of(lax.rem(x + d, 4) * OWN, OWN), OWN)
        ref[...] = (keep[rows, :] + got[rows, :].astype(F32)).astype(ref.dtype)


def split(keep, got):
    piece = jax.ShapeDtypeStruct((OWN, D), BF16)
    return pl.pallas_call(
        split_body,
        out_shape=(jax.ShapeDtypeStruct((OWN, D), F32), piece, piece, piece),
        in_specs=[vmem_spec()] * 2,
        out_specs=(vmem_spec(),) * 4,
        compiler_params=params(12),
        name="split",
    )(keep, got)


def middle_body(picked, own, r1, r2, r3, gain, attention, normed):
    total = own[...] + r1[...].astype(F32) + r2[...].astype(F32) + r3[...].astype(F32)
    attention[...] = total
    mid = (picked[...].astype(F32) + total).astype(BF16).astype(F32)
    inv = lax.rsqrt(jnp.mean(mid * mid, axis=1, keepdims=True) + EPS)
    normed[...] = (mid * inv * gain[...]).astype(BF16)


def middle(picked, own, got, gain):
    return pl.pallas_call(
        middle_body,
        out_shape=(jax.ShapeDtypeStruct((OWN, D), F32), jax.ShapeDtypeStruct((OWN, D), BF16)),
        in_specs=[vmem_spec()] * 6,
        out_specs=(vmem_spec(),) * 2,
        compiler_params=params(12),
        name="middle",
    )(picked, own, *got, gain)


def feed_body(*refs):
    place = refs[0]
    xs = refs[1:5]
    pieces = refs[5:13]
    outs = refs[13:17]
    tokens, gate, up, down, hidden, acted, sems = refs[17:]
    copies = [[], [], []]
    for e, x in enumerate(xs):
        copies[0].append(pltpu.make_async_copy(x, tokens.at[e * 128:(e + 1) * 128, :], sems.at[e]))
    for k, weight in enumerate((gate, up, down)):
        for i in range(16):
            rows = pl.ds(pl.multiple_of(place[i] * ROWS, 16), ROWS)
            at = (3 * (i % 2) + k) * ROWS
            copies[k].append(pltpu.make_async_copy(pieces[i // 2].at[at:at + ROWS, :], weight.at[rows, :],
                                                   sems.at[4 + 16 * k + i]))
    for copy in copies[0]:
        copy.start()
    chunks = [slice(j * 256, min((j + 1) * 256, FF_DEV)) for j in range(5)]
    for copy in copies[0]:
        copy.wait()
    for copy in copies[1]:
        copy.start()
    for cols in chunks:
        one = jnp.dot(tokens[...], gate[:, cols], preferred_element_type=F32)
        acted[:, cols] = one / (1.0 + jnp.exp(-one))
    for copy in copies[1]:
        copy.wait()
    for copy in copies[2]:
        copy.start()
    for cols in chunks:
        two = jnp.dot(tokens[...], up[:, cols], preferred_element_type=F32)
        hidden[:, cols] = (acted[:, cols] * two).astype(BF16)
    for copy in copies[2]:
        copy.wait()
    for n in range(D // 256):
        rows = slice(n * 256, (n + 1) * 256)
        part = lax.dot_general(hidden[...], down[rows, :], (((1,), (1,)), ((), ())),
                               preferred_element_type=F32).astype(BF16)
        for e, out in enumerate(outs):
            out[:, rows] = part[e * 128:(e + 1) * 128, :]


def feed(place, xs, pieces):
    return pl.pallas_call(
        feed_body,
        out_shape=(jax.ShapeDtypeStruct((4 * OWN, D), BF16),) * 4,
        in_specs=[smem_spec()] + [hbm_spec()] * 12,
        out_specs=(vmem_spec(),) * 4,
        scratch_shapes=[pltpu.VMEM((512, D), BF16), pltpu.VMEM((D, FF_DEV), BF16), pltpu.VMEM((D, FF_DEV), BF16),
                        pltpu.VMEM((D, FF_DEV), BF16), pltpu.VMEM((512, FF_DEV), BF16), pltpu.VMEM((512, FF_DEV), F32),
                        pltpu.SemaphoreType.DMA((52,))],
        compiler_params=params(60),
        name="feed",
    )(place, *xs, *pieces)


def fold_body(p0, p1, p2, p3, own, s1, s2, s3):
    for d, out in enumerate((own, s1, s2, s3)):
        rows = slice(d * OWN, (d + 1) * OWN)
        total = p0[rows, :].astype(F32) + p1[rows, :].astype(F32)
        out[...] = (total + p2[rows, :].astype(F32) + p3[rows, :].astype(F32)).astype(out.dtype)


def fold(parts):
    piece = jax.ShapeDtypeStruct((OWN, D), BF16)
    return pl.pallas_call(
        fold_body,
        out_shape=(jax.ShapeDtypeStruct((OWN, D), F32), piece, piece, piece),
        in_specs=[vmem_spec()] * 4,
        out_specs=(vmem_spec(),) * 4,
        compiler_params=params(12),
        name="fold",
    )(*parts)


def finish_body(picked, attention, gate, own, r1, r2, r3, out):
    total = attention[...] + own[...]
    total = total + r1[...].astype(F32) + r2[...].astype(F32) + r3[...].astype(F32)
    out[...] = (picked[...].astype(F32) + gate[...] * total).astype(BF16)


def finish(picked, attention, gate, parts):
    return pl.pallas_call(
        finish_body,
        out_shape=jax.ShapeDtypeStruct((OWN, D), BF16),
        in_specs=[vmem_spec()] * 7,
        out_specs=vmem_spec(),
        compiler_params=params(12),
        name="finish",
    )(picked, attention, gate, *parts)


def merge_body(first, second, out, sems):
    copies = [pltpu.make_async_copy(ref, out.at[s * 3 * ROWS:(s + 1) * 3 * ROWS, :], sems.at[s])
              for s, ref in enumerate((first, second))]
    for copy in copies:
        copy.start()
    for copy in copies:
        copy.wait()


def merge(first, second):
    return pl.pallas_call(
        merge_body,
        out_shape=jax.ShapeDtypeStruct((6 * ROWS, FF_DEV), BF16),
        in_specs=[hbm_spec()] * 2,
        out_specs=vmem_spec(),
        scratch_shapes=[pltpu.SemaphoreType.DMA((2,))],
        compiler_params=params(60),
        name="merge",
    )(first, second)


def join_body(*refs):
    for i, ref in enumerate(refs[:4]):
        refs[4][i * OWN:(i + 1) * OWN, :] = ref[...]


def join(pieces):
    return pl.pallas_call(
        join_body,
        out_shape=jax.ShapeDtypeStruct((4 * OWN, D), BF16),
        in_specs=[vmem_spec()] * 4,
        out_specs=vmem_spec(),
        compiler_params=params(12),
        name="join",
    )(*pieces)


def hold_body(block, out, sem):
    copy = pltpu.make_async_copy(block, out, sem)
    copy.start()
    copy.wait()


def hold(block):
    return pl.pallas_call(
        hold_body,
        out_shape=jax.ShapeDtypeStruct((SEQ_DEV, D), BF16),
        in_specs=[hbm_spec()],
        out_specs=vmem_spec(),
        scratch_shapes=[pltpu.SemaphoreType.DMA],
        compiler_params=params(20),
        name="hold",
    )(block)


def place_body(occupied, chosen, block, *refs):
    pieces = refs[:2]
    out = refs[2]
    rows = refs[3]

    @pl.when(pl.program_id(0) == 0)
    def _():
        for core, piece in enumerate(pieces):
            for dx in range(4):
                at = lax.rem(lax.axis_index("c") + core, 2) * 128 + lax.rem(lax.axis_index("x") + 4 - dx, 4) * OWN
                rows[pl.ds(pl.multiple_of(at, OWN), OWN), :] = piece[dx * OWN:(dx + 1) * OWN, :]

    position = lax.broadcasted_iota(jnp.int32, (STEP, CAP), 0) + pl.program_id(0) * STEP
    slot = lax.broadcasted_iota(jnp.int32, (STEP, CAP), 1)
    hit = jnp.where((position == chosen[...]) & (slot < occupied[0]), 1.0, 0.0)
    taken = jnp.sum(hit, axis=1, keepdims=True) > 0.5
    hit = hit.astype(BF16)
    for n in range(D // 256):
        cols = slice(n * 256, (n + 1) * 256)
        new = jnp.dot(hit, rows[:, cols], preferred_element_type=F32).astype(BF16)
        out[:, cols] = jnp.where(taken, new, block[:, cols])


def put_back(occupied, chosen, block, pieces):
    return pl.pallas_call(
        place_body,
        grid=(SEQ_DEV // STEP,),
        out_shape=jax.ShapeDtypeStruct((SEQ_DEV, D), BF16),
        in_specs=[smem_spec(), pl.BlockSpec((1, CAP), lambda i: (0, 0)),
                  pl.BlockSpec((STEP, D), lambda i: (i, 0))]
        + [pl.BlockSpec((128, D), lambda i: (0, 0))] * 2,
        out_specs=pl.BlockSpec((STEP, D), lambda i: (i, 0)),
        scratch_shapes=[pltpu.VMEM((CAP, D), BF16)],
        compiler_params=params(20),
        name="put_back",
    )(occupied, chosen, block, *pieces)


def shift(value, axis, step, size=4):
    return lax.ppermute(value, axis, [(i, (i + step) % size) for i in range(size)])


def cross(value, step, first):
    pairs = []
    for y in range(4):
        for x in range(4):
            for c in range(2):
                along_x = (c == 0) == first
                to_y, to_x = (y, (x + step) % 4) if along_x else ((y + step) % 4, x)
                pairs.append((8 * y + 2 * x + c, 8 * to_y + 2 * to_x + c))
    return lax.ppermute(value, ("y", "x", "c"), pairs)


def around(value, step):
    pairs = [(2 * z + c, 2 * ((z + (step if c == 0 else 4 - step)) % 4) + c) for z in range(4) for c in range(2)]
    return lax.ppermute(value, ("z", "c"), pairs)


def swap(value):
    return shift(value, "c", 1, 2)


def weight_pairs(s):
    return [(2 * sy + sc, 2 * (2 * sc + (sy + s) % 2) + sy // 2) for sy in range(4) for sc in range(2)]


def tie(*values):
    return lax.optimization_barrier(values)


def local(block, preference, chosen, occupied, gain1, wq, wk, wv, wo, sharpness, gain2, gate_w, up_w, down_w):
    y, z, x, c = (lax.axis_index(n) for n in ("y", "z", "x", "c"))
    own_at = c * 128 + x * OWN
    near = 3 - 2 * c
    place = []
    for core, step in ((c, near), (1 - c, 4 - near)):
        for source in (z, z + step, z + 4 - step, z + 2):
            for s in range(2):
                place.append(4 * (2 * core + (y + s) % 2) + source % 4)
    place = jnp.stack(place).astype(jnp.int32)

    frequency = 10000.0 ** (-(np.arange(HD) % (HD // 2)) / (HD // 2))
    frequency = jnp.asarray(frequency.astype(np.float32)[None, :])
    packs = pack(gate_w, up_w, down_w)
    *packs, occupied = tie(*packs, occupied)
    got = [lax.ppermute(p, ("y", "c"), weight_pairs(s)) for s, p in enumerate(packs)]
    q, kv, picked = begin(occupied, block, chosen[None, :], gain1[None, :], frequency, wq, wk, wv)

    kv = lax.all_to_all(kv, "z", 0, 0)
    asked = [shift(q, "y", d) for d in (1, 2, 3)]
    merged = merge(*got)
    kv, *asked, merged = tie(kv, *asked, merged)
    near = around(merged, 1)

    scale = sharpness * (LOG2E / math.sqrt(HD))
    parts = []
    for d in (1, 2, 3):
        at = jnp.broadcast_to(jnp.where((y - d) % 4 > y, CAP, -CAP), (4,)).astype(jnp.int32)
        parts.append(shift(attend(False, at, scale, asked[d - 1], kv), "y", 4 - d))
    at = jnp.stack([jnp.where(j < z, CAP, jnp.where(j == z, 0, -CAP)) for j in range(4)]).astype(jnp.int32)
    parts.append(attend(True, at, scale, q, kv))

    *parts, near, merged = tie(*parts, near, merged)
    side = around(merged, 3)
    keep, send = mix(parts, wo)
    others = [swap(piece) for piece in (merged, near, side)]
    met, others[0] = tie(swap(send), others[0])
    own, s1, s2, s3 = split(keep, met)
    moved = [shift(s, "x", d) for d, s in ((1, s1), (2, s2), (3, s3))]
    *moved, others[1], near = tie(*moved, others[1], near)
    far = around(near, 1)
    attention, normed = middle(picked, own, moved, gain2[None, :])

    moved = [cross(normed, d, True) for d in (1, 2, 3)]
    *moved, side = tie(*moved, side)
    others[2] = swap(side)
    row = join([normed] + moved)
    xs = [row] + [cross(row, e, False) for e in (1, 2, 3)]
    *xs, others[2], far = tie(*xs, others[2], far)
    others.append(swap(far))
    outs = feed(place, xs, [merged, near, side, far] + others)
    own, s1, s2, s3 = fold([outs[0]] + [cross(outs[e], 4 - e, False) for e in (1, 2, 3)])
    outs = [own] + [cross(s, 4 - d, True) for d, s in ((1, s1), (2, s2), (3, s3))]

    mine = lax.dynamic_slice_in_dim(chosen, own_at, OWN, 0)
    hit = mine[:, None] == jnp.arange(SEQ_DEV, dtype=jnp.int32)[None, :]
    router = jax.nn.sigmoid(jnp.sum(jnp.where(hit, preference[None, :], 0.0), axis=1, keepdims=True))
    result = finish(picked, attention, router, outs)
    *rows, block = tie(*[shift(result, "x", d) for d in (1, 2, 3)], hold(block))
    rows = join([result] + rows)
    return put_back(occupied, chosen[None, :], block, [rows, swap(rows)])


def solution(mesh):
    grid = Mesh(mesh.devices.reshape(4, 4, 4, 2), ("y", "z", "x", "c"))
    ctx, mp = ("y", "z"), ("x", "c")
    return jax.shard_map(
        local,
        mesh=grid,
        in_specs=(P(ctx, None), P(ctx), P(ctx), P(ctx), P(), P(None, mp), P(None, mp), P(None, mp),
                  P(mp, None), P(mp), P(), P(ctx, mp), P(ctx, mp), P(ctx, mp)),
        out_specs=P(ctx, None),
        check_vma=False,
    )
```

```python
import functools
import math

import jax
import jax.numpy as jnp
from jax import lax
from jax.experimental import pallas as pl
from jax.experimental.pallas import tpu as pltpu
from jax.sharding import Mesh, PartitionSpec as P
import numpy as np

D = 2304
CAP = 256
SEQ_DEV = 1024
HD = 128
FF_DEV = 1152
ROWS = 144
STEP = 512
OWN = 32
EPS = 1e-06
NEG = -1e30
LOG2E = 1.4426950408889634
MB = 1024 * 1024
F32 = jnp.float32
BF16 = jnp.bfloat16


def vmem_spec():
    return pl.BlockSpec(memory_space=pltpu.VMEM)


def smem_spec():
    return pl.BlockSpec(memory_space=pltpu.SMEM)


def hbm_spec():
    return pl.BlockSpec(memory_space=pltpu.HBM)


def params(mib):
    return pltpu.CompilerParams(vmem_limit_bytes=mib * MB)


def begin_body(occupied, block_hbm, chosen, gain, frequency, wq_hbm, wk_hbm, wv_hbm,
               q_out, kv_hbm, own_out, block, picked, normed, wq, wk, wv, kv_out, sems):
    tiles = D // 256
    loads = [pltpu.make_async_copy(block_hbm.at[:, i * 256:(i + 1) * 256],
                                   block.at[:, i * 256:(i + 1) * 256], sems.at[i])
             for i in range(tiles)]
    weights = [pltpu.make_async_copy(src, dst, sems.at[9 + i])
               for i, (src, dst) in enumerate(((wk_hbm, wk), (wv_hbm, wv), (wq_hbm, wq)))]
    for copy in loads:
        copy.start()
    wide = jnp.broadcast_to(chosen[...].astype(F32), (128, CAP))
    column = jnp.transpose(wide)[:, 0:1].astype(jnp.int32)
    shard = 4 * lax.axis_index("y") + lax.axis_index("z")
    angles = (column + shard * SEQ_DEV).astype(F32) * frequency[...]
    cosine, sine = jnp.cos(angles), jnp.sin(angles)
    sine = jnp.where(lax.broadcasted_iota(jnp.int32, (CAP, HD), 1) < HD // 2, -sine, sine)
    lanes = lax.broadcasted_iota(jnp.int32, (CAP, SEQ_DEV), 1)
    one_hot = jnp.where(lanes == column, 1.0, 0.0).astype(BF16)
    total = jnp.zeros((CAP, 256), F32)
    for i in range(tiles):
        cols = slice(i * 256, (i + 1) * 256)
        loads[i].wait()
        if i == 4:
            for copy in weights:
                copy.start()
        part = jnp.dot(one_hot, block[:, cols], preferred_element_type=F32)
        picked[:, cols] = part.astype(BF16)
        total = total + part * part
    inv = lax.rsqrt(jnp.sum(total, axis=1, keepdims=True) / D + EPS)
    for i in range(tiles):
        cols = slice(i * 256, (i + 1) * 256)
        normed[:, cols] = (picked[:, cols].astype(F32) * inv * gain[:, cols]).astype(BF16)
    first = lax.axis_index("c") * 128 + lax.axis_index("x") * OWN
    own_out[...] = picked[pl.ds(pl.multiple_of(first, OWN), OWN), :]

    def turn(values):
        return values * cosine + pltpu.roll(values, HD // 2, 1) * sine

    weights[0].wait()
    keys = jnp.dot(normed[...], wk[...], preferred_element_type=F32)
    for h in range(2):
        kv_out[h * HD:(h + 1) * HD, 0:CAP] = jnp.transpose(turn(keys[:, h * HD:(h + 1) * HD])).astype(BF16)
    weights[1].wait()
    kv_out[0:CAP, 256:512] = jnp.dot(normed[...], wv[...], preferred_element_type=F32).astype(BF16)
    kv_out[CAP:CAP + 16, :] = jnp.full((16, 512), occupied[0].astype(F32), F32).astype(BF16)
    stores = [pltpu.make_async_copy(kv_out, kv_hbm.at[n], sems.at[n]) for n in range(4)]
    for copy in stores:
        copy.start()
    weights[2].wait()
    for j in range(2):
        part = jnp.dot(normed[...], wq[:, j * 256:(j + 1) * 256], preferred_element_type=F32)
        for h in range(2):
            at = j * 256 + h * HD
            q_out[:, at:at + HD] = turn(part[:, h * HD:(h + 1) * HD]).astype(BF16)
    for copy in stores:
        copy.wait()


def begin(occupied, block, chosen, gain, frequency, wq, wk, wv):
    return pl.pallas_call(
        begin_body,
        out_shape=(jax.ShapeDtypeStruct((CAP, 512), BF16), jax.ShapeDtypeStruct((4, CAP + 16, 512), BF16),
                   jax.ShapeDtypeStruct((OWN, D), BF16)),
        in_specs=[smem_spec(), hbm_spec()] + [vmem_spec()] * 3 + [hbm_spec()] * 3,
        out_specs=(vmem_spec(), hbm_spec(), vmem_spec()),
        scratch_shapes=[pltpu.VMEM((SEQ_DEV, D), BF16), pltpu.VMEM((CAP, D), BF16), pltpu.VMEM((CAP, D), BF16),
                        pltpu.VMEM((D, 512), BF16), pltpu.VMEM((D, 256), BF16), pltpu.VMEM((D, 256), BF16),
                        pltpu.VMEM((CAP + 16, 512), BF16),
                        pltpu.SemaphoreType.DMA((12,))],
        compiler_params=params(60),
        name="begin",
    )(occupied, block, chosen, gain, frequency, wq, wk, wv)


def pack_body(gate, up, down, out0, out1, packed, sems):
    loads, stores = [], []
    for s, out in enumerate((out0, out1)):
        cols = pl.ds(pl.multiple_of(lax.rem(lax.axis_index("y") + s, 2) * FF_DEV, FF_DEV), FF_DEV)
        for k, weight in enumerate((gate, up, down)):
            rows = slice(k * ROWS, (k + 1) * ROWS)
            at = 3 * s + k
            loads.append(pltpu.make_async_copy(weight.at[:, cols], packed.at[s, rows, :], sems.at[at]))
            stores.append(pltpu.make_async_copy(packed.at[s, rows, :], out.at[rows, :], sems.at[6 + at]))
    for load in loads:
        load.start()
    for load, store in zip(loads, stores):
        load.wait()
        store.start()
    for store in stores:
        store.wait()


def pack(gate, up, down):
    return pl.pallas_call(
        pack_body,
        out_shape=(jax.ShapeDtypeStruct((3 * ROWS, FF_DEV), BF16),) * 2,
        in_specs=[hbm_spec()] * 3,
        out_specs=(hbm_spec(),) * 2,
        scratch_shapes=[pltpu.VMEM((2, 3 * ROWS, FF_DEV), BF16), pltpu.SemaphoreType.DMA((12,))],
        compiler_params=params(60),
        name="pack",
    )(gate, up, down)


def attend_body(diagonal, at, scale, q, kv, out, stats):
    lane = lax.broadcasted_iota(jnp.int32, (1, CAP), 1).astype(F32)
    bias = []
    for j in range(4):
        count = kv[j, CAP:CAP + 16, 0:CAP].astype(F32)[0:1, :]
        live = (lane < count) & (at[j] >= 0)
        bias.append(jnp.where(live, 0.0, NEG))
    past = lax.broadcasted_iota(jnp.int32, (CAP, CAP), 1) - lax.broadcasted_iota(jnp.int32, (CAP, CAP), 0)
    for head in range(4):
        g = head // 2
        cols = slice(head * HD, (head + 1) * HD)
        query = q[:, cols]
        scores = []
        for j in range(4):
            part = jnp.dot(query, kv[j, g * HD:(g + 1) * HD, 0:CAP], preferred_element_type=F32)
            part = part * scale[head] + bias[j]
            if diagonal:
                part = jnp.where(past <= at[j], part, NEG)
            scores.append(part)
        top = jnp.max(functools.reduce(jnp.maximum, scores), axis=1, keepdims=True)
        weights = [jnp.exp2(part - top) for part in scores]
        total = jnp.sum(functools.reduce(jnp.add, weights), axis=1, keepdims=True)
        mixed = jnp.zeros((CAP, HD), F32)
        for j in range(4):
            mixed = mixed + jnp.dot(weights[j].astype(BF16), kv[j, 0:CAP, 256 + g * HD:256 + (g + 1) * HD],
                                    preferred_element_type=F32)
        out[0:CAP, cols] = (mixed * (1.0 / total)).astype(BF16)
        log_sum = top + jnp.log2(total)
        first = log_sum.astype(BF16).astype(F32)
        second = (log_sum - first).astype(BF16).astype(F32)
        stats[:, head:head + 1] = first
        stats[:, 4 + head:5 + head] = second
        stats[:, 8 + head:9 + head] = log_sum - first - second
    lanes = lax.broadcasted_iota(jnp.int32, (CAP, 128), 1)
    clean = jnp.where(lanes < 12, stats[...], 0.0)
    out[CAP:CAP + 16, 0:CAP] = jnp.transpose(clean)[0:16, :].astype(BF16)
    out[CAP:CAP + 16, CAP:512] = jnp.zeros((16, 512 - CAP), BF16)


def attend(diagonal, at, scale, q, kv):
    return pl.pallas_call(
        functools.partial(attend_body, diagonal),
        out_shape=jax.ShapeDtypeStruct((CAP + 16, 512), BF16),
        in_specs=[smem_spec()] * 2 + [vmem_spec()] * 2,
        out_specs=vmem_spec(),
        scratch_shapes=[pltpu.VMEM((CAP, 128), F32)],
        compiler_params=params(12),
        name="attend",
    )(at, scale, q, kv)


def mix_body(p0, p1, p2, p3, wo_hbm, keep, send, mixed, wo, sem):
    load = pltpu.make_async_copy(wo_hbm, wo, sem)
    load.start()
    parts = (p0, p1, p2, p3)
    logs = []
    for part in parts:
        rows = part[CAP:CAP + 16, 0:CAP].astype(F32)
        rows = jnp.concatenate([rows, jnp.zeros((112, CAP), F32)], axis=0)
        logs.append(jnp.transpose(rows))
    for head in range(4):
        cols = slice(head * HD, (head + 1) * HD)
        each = [log[:, head:head + 1] + log[:, 4 + head:5 + head] + log[:, 8 + head:9 + head] for log in logs]
        top = functools.reduce(jnp.maximum, each)
        weights = [jnp.exp2(one - top) for one in each]
        total = functools.reduce(jnp.add, weights)
        value = functools.reduce(jnp.add, [w * part[0:CAP, cols].astype(F32) for w, part in zip(weights, parts)])
        mixed[:, cols] = (value / total).astype(BF16)
    core = lax.axis_index("c")
    mine = mixed[pl.ds(pl.multiple_of(core * 128, 128), 128), :]
    other = mixed[pl.ds(pl.multiple_of((1 - core) * 128, 128), 128), :]

    load.wait()
    for i in range(D // 256):
        cols = slice(i * 256, (i + 1) * 256)
        send[:, cols] = jnp.dot(other, wo[:, cols], preferred_element_type=F32).astype(BF16)
        keep[:, cols] = jnp.dot(mine, wo[:, cols], preferred_element_type=F32)


def mix(parts, wo):
    return pl.pallas_call(
        mix_body,
        out_shape=(jax.ShapeDtypeStruct((128, D), F32), jax.ShapeDtypeStruct((128, D), BF16)),
        in_specs=[vmem_spec()] * 4 + [hbm_spec()],
        out_specs=(vmem_spec(),) * 2,
        scratch_shapes=[pltpu.VMEM((CAP, 512), BF16), pltpu.VMEM((512, D), BF16), pltpu.SemaphoreType.DMA],
        compiler_params=params(16),
        name="mix",
    )(*parts, wo)


def split_body(keep, got, own, s1, s2, s3):
    x = lax.axis_index("x")
    for d, ref in enumerate((own, s1, s2, s3)):
        rows = pl.ds(pl.multiple_of(lax.rem(x + d, 4) * OWN, OWN), OWN)
        ref[...] = (keep[rows, :] + got[rows, :].astype(F32)).astype(ref.dtype)


def split(keep, got):
    piece = jax.ShapeDtypeStruct((OWN, D), BF16)
    return pl.pallas_call(
        split_body,
        out_shape=(jax.ShapeDtypeStruct((OWN, D), F32), piece, piece, piece),
        in_specs=[vmem_spec()] * 2,
        out_specs=(vmem_spec(),) * 4,
        compiler_params=params(12),
        name="split",
    )(keep, got)


def middle_body(picked, own, r1, r2, r3, gain, attention, normed):
    total = own[...] + r1[...].astype(F32) + r2[...].astype(F32) + r3[...].astype(F32)
    attention[...] = total
    mid = (picked[...].astype(F32) + total).astype(BF16).astype(F32)
    inv = lax.rsqrt(jnp.mean(mid * mid, axis=1, keepdims=True) + EPS)
    normed[...] = (mid * inv * gain[...]).astype(BF16)


def middle(picked, own, got, gain):
    return pl.pallas_call(
        middle_body,
        out_shape=(jax.ShapeDtypeStruct((OWN, D), F32), jax.ShapeDtypeStruct((OWN, D), BF16)),
        in_specs=[vmem_spec()] * 6,
        out_specs=(vmem_spec(),) * 2,
        compiler_params=params(12),
        name="middle",
    )(picked, own, *got, gain)


def feed_body(*refs):
    xs = refs[0:4]
    pieces = refs[4:12]
    outs = refs[12:16]
    tokens, gate, up, down, hidden, acted, sems = refs[16:]
    y, z, c = (lax.axis_index(n) for n in ("y", "z", "c"))
    near = 3 - 2 * c
    place = []
    for core, step in ((c, near), (1 - c, 4 - near)):
        for source in (z, z + step, z + 4 - step, z + 2):
            for s in range(2):
                place.append(4 * (2 * core + lax.rem(y + s, 2)) + lax.rem(source, 4))
    copies = [[], [], []]
    for e, x in enumerate(xs):
        copies[0].append(pltpu.make_async_copy(x, tokens.at[e * 128:(e + 1) * 128, :], sems.at[e]))
    for k, weight in enumerate((gate, up, down)):
        for i in range(16):
            rows = pl.ds(pl.multiple_of(place[i] * ROWS, 16), ROWS)
            at = (3 * (i % 2) + k) * ROWS
            copies[k].append(pltpu.make_async_copy(pieces[i // 2].at[at:at + ROWS, :], weight.at[rows, :],
                                                   sems.at[4 + 16 * k + i]))
    for copy in copies[0]:
        copy.start()
    chunks = [slice(j * 256, min((j + 1) * 256, FF_DEV)) for j in range(5)]
    for copy in copies[0]:
        copy.wait()
    for copy in copies[1]:
        copy.start()
    for cols in chunks:
        one = jnp.dot(tokens[...], gate[:, cols], preferred_element_type=F32)
        acted[:, cols] = one / (1.0 + jnp.exp(-one))
    for copy in copies[1]:
        copy.wait()
    for copy in copies[2]:
        copy.start()
    for cols in chunks:
        two = jnp.dot(tokens[...], up[:, cols], preferred_element_type=F32)
        hidden[:, cols] = (acted[:, cols] * two).astype(BF16)
    for copy in copies[2]:
        copy.wait()
    for n in range(D // 256):
        rows = slice(n * 256, (n + 1) * 256)
        part = lax.dot_general(hidden[...], down[rows, :], (((1,), (1,)), ((), ())),
                               preferred_element_type=F32).astype(BF16)
        for e, out in enumerate(outs):
            out[:, rows] = part[e * 128:(e + 1) * 128, :]


def feed(xs, pieces):
    return pl.pallas_call(
        feed_body,
        out_shape=(jax.ShapeDtypeStruct((4 * OWN, D), BF16),) * 4,
        in_specs=[hbm_spec()] * 12,
        out_specs=(vmem_spec(),) * 4,
        scratch_shapes=[pltpu.VMEM((512, D), BF16), pltpu.VMEM((D, FF_DEV), BF16), pltpu.VMEM((D, FF_DEV), BF16),
                        pltpu.VMEM((D, FF_DEV), BF16), pltpu.VMEM((512, FF_DEV), BF16), pltpu.VMEM((512, FF_DEV), F32),
                        pltpu.SemaphoreType.DMA((52,))],
        compiler_params=params(60),
        name="feed",
    )(*xs, *pieces)


def fold_body(p0, p1, p2, p3, own, s1, s2, s3):
    for d, out in enumerate((own, s1, s2, s3)):
        rows = slice(d * OWN, (d + 1) * OWN)
        total = p0[rows, :].astype(F32) + p1[rows, :].astype(F32)
        out[...] = (total + p2[rows, :].astype(F32) + p3[rows, :].astype(F32)).astype(out.dtype)


def fold(parts):
    piece = jax.ShapeDtypeStruct((OWN, D), BF16)
    return pl.pallas_call(
        fold_body,
        out_shape=(jax.ShapeDtypeStruct((OWN, D), F32), piece, piece, piece),
        in_specs=[vmem_spec()] * 4,
        out_specs=(vmem_spec(),) * 4,
        compiler_params=params(12),
        name="fold",
    )(*parts)


def finish_body(picked, attention, gate, own, r1, r2, r3, out):
    total = attention[...] + own[...]
    total = total + r1[...].astype(F32) + r2[...].astype(F32) + r3[...].astype(F32)
    out[...] = (picked[...].astype(F32) + gate[...] * total).astype(BF16)


def finish(picked, attention, gate, parts):
    return pl.pallas_call(
        finish_body,
        out_shape=jax.ShapeDtypeStruct((OWN, D), BF16),
        in_specs=[vmem_spec()] * 7,
        out_specs=vmem_spec(),
        compiler_params=params(12),
        name="finish",
    )(picked, attention, gate, *parts)


def merge_body(first, second, out, sems):
    copies = [pltpu.make_async_copy(ref, out.at[s * 3 * ROWS:(s + 1) * 3 * ROWS, :], sems.at[s])
              for s, ref in enumerate((first, second))]
    for copy in copies:
        copy.start()
    for copy in copies:
        copy.wait()


def merge(first, second):
    return pl.pallas_call(
        merge_body,
        out_shape=jax.ShapeDtypeStruct((6 * ROWS, FF_DEV), BF16),
        in_specs=[hbm_spec()] * 2,
        out_specs=vmem_spec(),
        scratch_shapes=[pltpu.SemaphoreType.DMA((2,))],
        compiler_params=params(60),
        name="merge",
    )(first, second)


def join_body(*refs):
    for i, ref in enumerate(refs[:4]):
        refs[4][i * OWN:(i + 1) * OWN, :] = ref[...]


def join(pieces):
    return pl.pallas_call(
        join_body,
        out_shape=jax.ShapeDtypeStruct((4 * OWN, D), BF16),
        in_specs=[vmem_spec()] * 4,
        out_specs=vmem_spec(),
        compiler_params=params(12),
        name="join",
    )(*pieces)


def hold_body(block, out, sem):
    copy = pltpu.make_async_copy(block, out, sem)
    copy.start()
    copy.wait()


def hold(block):
    return pl.pallas_call(
        hold_body,
        out_shape=jax.ShapeDtypeStruct((SEQ_DEV, D), BF16),
        in_specs=[hbm_spec()],
        out_specs=vmem_spec(),
        scratch_shapes=[pltpu.SemaphoreType.DMA],
        compiler_params=params(20),
        name="hold",
    )(block)


def place_body(occupied, chosen, block, *refs):
    pieces = refs[:2]
    out = refs[2]
    rows = refs[3]

    @pl.when(pl.program_id(0) == 0)
    def _():
        for core, piece in enumerate(pieces):
            for dx in range(4):
                at = lax.rem(lax.axis_index("c") + core, 2) * 128 + lax.rem(lax.axis_index("x") + 4 - dx, 4) * OWN
                rows[pl.ds(pl.multiple_of(at, OWN), OWN), :] = piece[dx * OWN:(dx + 1) * OWN, :]

    position = lax.broadcasted_iota(jnp.int32, (STEP, CAP), 0) + pl.program_id(0) * STEP
    slot = lax.broadcasted_iota(jnp.int32, (STEP, CAP), 1)
    hit = jnp.where((position == chosen[...]) & (slot < occupied[0]), 1.0, 0.0)
    taken = jnp.sum(hit, axis=1, keepdims=True) > 0.5
    hit = hit.astype(BF16)
    for n in range(D // 256):
        cols = slice(n * 256, (n + 1) * 256)
        new = jnp.dot(hit, rows[:, cols], preferred_element_type=F32).astype(BF16)
        out[:, cols] = jnp.where(taken, new, block[:, cols])


def put_back(occupied, chosen, block, pieces):
    return pl.pallas_call(
        place_body,
        grid=(SEQ_DEV // STEP,),
        out_shape=jax.ShapeDtypeStruct((SEQ_DEV, D), BF16),
        in_specs=[smem_spec(), pl.BlockSpec((1, CAP), lambda i: (0, 0)),
                  pl.BlockSpec((STEP, D), lambda i: (i, 0))]
        + [pl.BlockSpec((128, D), lambda i: (0, 0))] * 2,
        out_specs=pl.BlockSpec((STEP, D), lambda i: (i, 0)),
        scratch_shapes=[pltpu.VMEM((CAP, D), BF16)],
        compiler_params=params(20),
        name="put_back",
    )(occupied, chosen, block, *pieces)


def shift(value, axis, step, size=4):
    return lax.ppermute(value, axis, [(i, (i + step) % size) for i in range(size)])


def cross(value, step, first):
    pairs = []
    for y in range(4):
        for x in range(4):
            for c in range(2):
                along_x = (c == 0) == first
                to_y, to_x = (y, (x + step) % 4) if along_x else ((y + step) % 4, x)
                pairs.append((8 * y + 2 * x + c, 8 * to_y + 2 * to_x + c))
    return lax.ppermute(value, ("y", "x", "c"), pairs)


def around(value, step):
    pairs = [(2 * z + c, 2 * ((z + (step if c == 0 else 4 - step)) % 4) + c) for z in range(4) for c in range(2)]
    return lax.ppermute(value, ("z", "c"), pairs)


def swap(value):
    return shift(value, "c", 1, 2)


def weight_pairs(s):
    return [(2 * sy + sc, 2 * (2 * sc + (sy + s) % 2) + sy // 2) for sy in range(4) for sc in range(2)]


def tie(*values):
    return lax.optimization_barrier(values)


def local(block, preference, chosen, occupied, gain1, wq, wk, wv, wo, sharpness, gain2, gate_w, up_w, down_w):
    y, z, x, c = (lax.axis_index(n) for n in ("y", "z", "x", "c"))
    own_at = c * 128 + x * OWN
    frequency = 10000.0 ** (-(np.arange(HD) % (HD // 2)) / (HD // 2))
    frequency = jnp.asarray(frequency.astype(np.float32)[None, :])
    packs = pack(gate_w, up_w, down_w)
    *packs, occupied = tie(*packs, occupied)
    got = [lax.ppermute(p, ("y", "c"), weight_pairs(s)) for s, p in enumerate(packs)]
    q, kv, picked = begin(occupied, block, chosen[None, :], gain1[None, :], frequency, wq, wk, wv)

    kv = lax.all_to_all(kv, "z", 0, 0)
    asked = [shift(q, "y", d) for d in (1, 2, 3)]
    merged = merge(*got)
    kv, *asked, merged = tie(kv, *asked, merged)
    near = around(merged, 1)

    scale = sharpness * (LOG2E / math.sqrt(HD))
    parts = []
    for d in (1, 2, 3):
        at = jnp.broadcast_to(jnp.where((y - d) % 4 > y, CAP, -CAP), (4,)).astype(jnp.int32)
        parts.append(shift(attend(False, at, scale, asked[d - 1], kv), "y", 4 - d))
    at = jnp.stack([jnp.where(j < z, CAP, jnp.where(j == z, 0, -CAP)) for j in range(4)]).astype(jnp.int32)
    parts.append(attend(True, at, scale, q, kv))

    *parts, near, merged = tie(*parts, near, merged)
    side, far = around(merged, 3), around(near, 1)
    keep, send = mix(parts, wo)
    others = [swap(piece) for piece in (merged, near, side)]
    met, others[0] = tie(swap(send), others[0])
    own, s1, s2, s3 = split(keep, met)
    moved = [shift(s, "x", d) for d, s in ((1, s1), (2, s2), (3, s3))]
    *moved, others[1] = tie(*moved, others[1])
    attention, normed = middle(picked, own, moved, gain2[None, :])

    moved = [cross(normed, d, True) for d in (1, 2, 3)]
    *moved, side = tie(*moved, side)
    others[2] = swap(side)
    row = join([normed] + moved)
    xs = [row] + [cross(row, e, False) for e in (1, 2, 3)]
    *xs, others[2], far = tie(*xs, others[2], far)
    others.append(swap(far))
    outs = feed(xs, [merged, near, side, far] + others)
    own, s1, s2, s3 = fold([outs[0]] + [cross(outs[e], 4 - e, False) for e in (1, 2, 3)])
    outs = [own] + [cross(s, 4 - d, True) for d, s in ((1, s1), (2, s2), (3, s3))]

    mine = lax.dynamic_slice_in_dim(chosen, own_at, OWN, 0)
    hit = mine[:, None] == jnp.arange(SEQ_DEV, dtype=jnp.int32)[None, :]
    router = jax.nn.sigmoid(jnp.sum(jnp.where(hit, preference[None, :], 0.0), axis=1, keepdims=True))
    result = finish(picked, attention, router, outs)
    *rows, block = tie(*[shift(result, "x", d) for d in (1, 2, 3)], hold(block))
    rows = join([result] + rows)
    return put_back(occupied, chosen[None, :], block, [rows, swap(rows)])


def solution(mesh):
    grid = Mesh(mesh.devices.reshape(4, 4, 4, 2), ("y", "z", "x", "c"))
    ctx, mp = ("y", "z"), ("x", "c")
    return jax.shard_map(
        local,
        mesh=grid,
        in_specs=(P(ctx, None), P(ctx), P(ctx), P(ctx), P(), P(None, mp), P(None, mp), P(None, mp),
                  P(mp, None), P(mp), P(), P(ctx, mp), P(ctx, mp), P(ctx, mp)),
        out_specs=P(ctx, None),
        check_vma=False,
    )
```

```python
import functools
import math

import jax
import jax.numpy as jnp
from jax import lax
from jax.experimental import pallas as pl
from jax.experimental.pallas import tpu as pltpu
from jax.sharding import Mesh, PartitionSpec as P
import numpy as np

D = 2304
CAP = 256
SEQ_DEV = 1024
HD = 128
FF_DEV = 1152
ROWS = 144
STEP = 512
OWN = 32
EPS = 1e-06
NEG = -1e30
LOG2E = 1.4426950408889634
MB = 1024 * 1024
F32 = jnp.float32
BF16 = jnp.bfloat16


def vmem_spec():
    return pl.BlockSpec(memory_space=pltpu.VMEM)


def smem_spec():
    return pl.BlockSpec(memory_space=pltpu.SMEM)


def hbm_spec():
    return pl.BlockSpec(memory_space=pltpu.HBM)


def params(mib):
    return pltpu.CompilerParams(vmem_limit_bytes=mib * MB)


def begin_body(occupied, block_hbm, chosen, gain, frequency, wq_hbm, wk_hbm, wv_hbm,
               q_out, kv_hbm, own_out, block, picked, normed, wq, wk, wv, kv_out, sems):
    tiles = D // 256
    loads = [pltpu.make_async_copy(block_hbm.at[:, i * 256:(i + 1) * 256],
                                   block.at[:, i * 256:(i + 1) * 256], sems.at[i])
             for i in range(tiles)]
    weights = [pltpu.make_async_copy(src, dst, sems.at[9 + i])
               for i, (src, dst) in enumerate(((wk_hbm, wk), (wv_hbm, wv), (wq_hbm, wq)))]
    for copy in loads:
        copy.start()
    wide = jnp.broadcast_to(chosen[...].astype(F32), (128, CAP))
    column = jnp.transpose(wide)[:, 0:1].astype(jnp.int32)
    shard = 4 * lax.axis_index("y") + lax.axis_index("z")
    angles = (column + shard * SEQ_DEV).astype(F32) * frequency[...]
    cosine, sine = jnp.cos(angles), jnp.sin(angles)
    sine = jnp.where(lax.broadcasted_iota(jnp.int32, (CAP, HD), 1) < HD // 2, -sine, sine)
    lanes = lax.broadcasted_iota(jnp.int32, (CAP, SEQ_DEV), 1)
    one_hot = jnp.where(lanes == column, 1.0, 0.0).astype(BF16)
    total = jnp.zeros((CAP, 256), F32)
    for i in range(tiles):
        cols = slice(i * 256, (i + 1) * 256)
        loads[i].wait()
        if i == 4:
            for copy in weights:
                copy.start()
        part = jnp.dot(one_hot, block[:, cols], preferred_element_type=F32)
        picked[:, cols] = part.astype(BF16)
        total = total + part * part
    inv = lax.rsqrt(jnp.sum(total, axis=1, keepdims=True) / D + EPS)
    for i in range(tiles):
        cols = slice(i * 256, (i + 1) * 256)
        normed[:, cols] = (picked[:, cols].astype(F32) * inv * gain[:, cols]).astype(BF16)
    first = lax.axis_index("c") * 128 + lax.axis_index("x") * OWN
    own_out[...] = picked[pl.ds(pl.multiple_of(first, OWN), OWN), :]

    def turn(values):
        return values * cosine + pltpu.roll(values, HD // 2, 1) * sine

    weights[0].wait()
    keys = jnp.dot(normed[...], wk[...], preferred_element_type=F32)
    for h in range(2):
        kv_out[h * HD:(h + 1) * HD, 0:CAP] = jnp.transpose(turn(keys[:, h * HD:(h + 1) * HD])).astype(BF16)
    weights[1].wait()
    kv_out[0:CAP, 256:512] = jnp.dot(normed[...], wv[...], preferred_element_type=F32).astype(BF16)
    kv_out[CAP:CAP + 16, :] = jnp.full((16, 512), occupied[0].astype(F32), F32).astype(BF16)
    stores = [pltpu.make_async_copy(kv_out, kv_hbm.at[n], sems.at[n]) for n in range(4)]
    for copy in stores:
        copy.start()
    weights[2].wait()
    for j in range(2):
        part = jnp.dot(normed[...], wq[:, j * 256:(j + 1) * 256], preferred_element_type=F32)
        for h in range(2):
            at = j * 256 + h * HD
            q_out[:, at:at + HD] = turn(part[:, h * HD:(h + 1) * HD]).astype(BF16)
    for copy in stores:
        copy.wait()


def begin(occupied, block, chosen, gain, frequency, wq, wk, wv):
    return pl.pallas_call(
        begin_body,
        out_shape=(jax.ShapeDtypeStruct((CAP, 512), BF16), jax.ShapeDtypeStruct((4, CAP + 16, 512), BF16),
                   jax.ShapeDtypeStruct((OWN, D), BF16)),
        in_specs=[smem_spec(), hbm_spec()] + [vmem_spec()] * 3 + [hbm_spec()] * 3,
        out_specs=(vmem_spec(), hbm_spec(), vmem_spec()),
        scratch_shapes=[pltpu.VMEM((SEQ_DEV, D), BF16), pltpu.VMEM((CAP, D), BF16), pltpu.VMEM((CAP, D), BF16),
                        pltpu.VMEM((D, 512), BF16), pltpu.VMEM((D, 256), BF16), pltpu.VMEM((D, 256), BF16),
                        pltpu.VMEM((CAP + 16, 512), BF16),
                        pltpu.SemaphoreType.DMA((12,))],
        compiler_params=params(60),
        name="begin",
    )(occupied, block, chosen, gain, frequency, wq, wk, wv)


def pack_body(gate, up, down, out0, out1, packed, sems):
    loads, stores = [], []
    for s, out in enumerate((out0, out1)):
        cols = pl.ds(pl.multiple_of(lax.rem(lax.axis_index("y") + s, 2) * FF_DEV, FF_DEV), FF_DEV)
        for k, weight in enumerate((gate, up, down)):
            rows = slice(k * ROWS, (k + 1) * ROWS)
            at = 3 * s + k
            loads.append(pltpu.make_async_copy(weight.at[:, cols], packed.at[s, rows, :], sems.at[at]))
            stores.append(pltpu.make_async_copy(packed.at[s, rows, :], out.at[rows, :], sems.at[6 + at]))
    for load in loads:
        load.start()
    for load, store in zip(loads, stores):
        load.wait()
        store.start()
    for store in stores:
        store.wait()


def pack(gate, up, down):
    return pl.pallas_call(
        pack_body,
        out_shape=(jax.ShapeDtypeStruct((3 * ROWS, FF_DEV), BF16),) * 2,
        in_specs=[hbm_spec()] * 3,
        out_specs=(hbm_spec(),) * 2,
        scratch_shapes=[pltpu.VMEM((2, 3 * ROWS, FF_DEV), BF16), pltpu.SemaphoreType.DMA((12,))],
        compiler_params=params(60),
        name="pack",
    )(gate, up, down)


def attend_body(diagonal, at, scale, q, kv, out, stats):
    lane = lax.broadcasted_iota(jnp.int32, (1, CAP), 1).astype(F32)
    bias = []
    for j in range(4):
        count = kv[j, CAP:CAP + 16, 0:CAP].astype(F32)[0:1, :]
        live = (lane < count) & (at[j] >= 0)
        bias.append(jnp.where(live, 0.0, NEG))
    past = lax.broadcasted_iota(jnp.int32, (CAP, CAP), 1) - lax.broadcasted_iota(jnp.int32, (CAP, CAP), 0)
    for head in range(4):
        g = head // 2
        cols = slice(head * HD, (head + 1) * HD)
        query = q[:, cols]
        scores = []
        for j in range(4):
            part = jnp.dot(query, kv[j, g * HD:(g + 1) * HD, 0:CAP], preferred_element_type=F32)
            part = part * scale[head] + bias[j]
            if diagonal:
                part = jnp.where(past <= at[j], part, NEG)
            scores.append(part)
        top = jnp.max(functools.reduce(jnp.maximum, scores), axis=1, keepdims=True)
        weights = [jnp.exp2(part - top) for part in scores]
        total = jnp.sum(functools.reduce(jnp.add, weights), axis=1, keepdims=True)
        mixed = jnp.zeros((CAP, HD), F32)
        for j in range(4):
            mixed = mixed + jnp.dot(weights[j].astype(BF16), kv[j, 0:CAP, 256 + g * HD:256 + (g + 1) * HD],
                                    preferred_element_type=F32)
        out[0:CAP, cols] = (mixed * (1.0 / total)).astype(BF16)
        log_sum = top + jnp.log2(total)
        first = log_sum.astype(BF16).astype(F32)
        second = (log_sum - first).astype(BF16).astype(F32)
        stats[:, head:head + 1] = first
        stats[:, 4 + head:5 + head] = second
        stats[:, 8 + head:9 + head] = log_sum - first - second
    lanes = lax.broadcasted_iota(jnp.int32, (CAP, 128), 1)
    clean = jnp.where(lanes < 12, stats[...], 0.0)
    out[CAP:CAP + 16, 0:CAP] = jnp.transpose(clean)[0:16, :].astype(BF16)
    out[CAP:CAP + 16, CAP:512] = jnp.zeros((16, 512 - CAP), BF16)


def attend(diagonal, at, scale, q, kv):
    return pl.pallas_call(
        functools.partial(attend_body, diagonal),
        out_shape=jax.ShapeDtypeStruct((CAP + 16, 512), BF16),
        in_specs=[smem_spec()] * 2 + [vmem_spec()] * 2,
        out_specs=vmem_spec(),
        scratch_shapes=[pltpu.VMEM((CAP, 128), F32)],
        compiler_params=params(12),
        name="attend",
    )(at, scale, q, kv)


def mix_body(p0, p1, p2, p3, wo_hbm, keep, send, mixed, wo, sem):
    load = pltpu.make_async_copy(wo_hbm, wo, sem)
    load.start()
    parts = (p0, p1, p2, p3)
    logs = []
    for part in parts:
        rows = part[CAP:CAP + 16, 0:CAP].astype(F32)
        rows = jnp.concatenate([rows, jnp.zeros((112, CAP), F32)], axis=0)
        logs.append(jnp.transpose(rows))
    for head in range(4):
        cols = slice(head * HD, (head + 1) * HD)
        each = [log[:, head:head + 1] + log[:, 4 + head:5 + head] + log[:, 8 + head:9 + head] for log in logs]
        top = functools.reduce(jnp.maximum, each)
        weights = [jnp.exp2(one - top) for one in each]
        total = functools.reduce(jnp.add, weights)
        value = functools.reduce(jnp.add, [w * part[0:CAP, cols].astype(F32) for w, part in zip(weights, parts)])
        mixed[:, cols] = (value / total).astype(BF16)
    core = lax.axis_index("c")
    mine = mixed[pl.ds(pl.multiple_of(core * 128, 128), 128), :]
    other = mixed[pl.ds(pl.multiple_of((1 - core) * 128, 128), 128), :]

    load.wait()
    for i in range(D // 256):
        cols = slice(i * 256, (i + 1) * 256)
        send[:, cols] = jnp.dot(other, wo[:, cols], preferred_element_type=F32).astype(BF16)
        keep[:, cols] = jnp.dot(mine, wo[:, cols], preferred_element_type=F32)


def mix(parts, wo):
    return pl.pallas_call(
        mix_body,
        out_shape=(jax.ShapeDtypeStruct((128, D), F32), jax.ShapeDtypeStruct((128, D), BF16)),
        in_specs=[vmem_spec()] * 4 + [hbm_spec()],
        out_specs=(vmem_spec(),) * 2,
        scratch_shapes=[pltpu.VMEM((CAP, 512), BF16), pltpu.VMEM((512, D), BF16), pltpu.SemaphoreType.DMA],
        compiler_params=params(16),
        name="mix",
    )(*parts, wo)


def split_body(keep, got, own, s1, s2, s3):
    x = lax.axis_index("x")
    for d, ref in enumerate((own, s1, s2, s3)):
        rows = pl.ds(pl.multiple_of(lax.rem(x + d, 4) * OWN, OWN), OWN)
        ref[...] = (keep[rows, :] + got[rows, :].astype(F32)).astype(ref.dtype)


def split(keep, got):
    piece = jax.ShapeDtypeStruct((OWN, D), BF16)
    return pl.pallas_call(
        split_body,
        out_shape=(jax.ShapeDtypeStruct((OWN, D), F32), piece, piece, piece),
        in_specs=[vmem_spec()] * 2,
        out_specs=(vmem_spec(),) * 4,
        compiler_params=params(12),
        name="split",
    )(keep, got)


def middle_body(picked, own, r1, r2, r3, gain, attention, normed):
    total = own[...] + r1[...].astype(F32) + r2[...].astype(F32) + r3[...].astype(F32)
    attention[...] = total
    mid = (picked[...].astype(F32) + total).astype(BF16).astype(F32)
    inv = lax.rsqrt(jnp.mean(mid * mid, axis=1, keepdims=True) + EPS)
    normed[...] = (mid * inv * gain[...]).astype(BF16)


def middle(picked, own, got, gain):
    return pl.pallas_call(
        middle_body,
        out_shape=(jax.ShapeDtypeStruct((OWN, D), F32), jax.ShapeDtypeStruct((OWN, D), BF16)),
        in_specs=[vmem_spec()] * 6,
        out_specs=(vmem_spec(),) * 2,
        compiler_params=params(12),
        name="middle",
    )(picked, own, *got, gain)


def feed_body(*refs):
    xs = refs[0:4]
    pieces = refs[4:12]
    outs = refs[12:16]
    tokens, gate, up, down, hidden, acted, sems = refs[16:]
    y, z, c = (lax.axis_index(n) for n in ("y", "z", "c"))
    near = 3 - 2 * c
    place = []
    for core, step in ((c, near), (1 - c, 4 - near)):
        for source in (z, z + step, z + 4 - step, z + 2):
            for s in range(2):
                place.append(4 * (2 * core + lax.rem(y + s, 2)) + lax.rem(source, 4))
    copies = [[], [], []]
    for e, x in enumerate(xs):
        copies[0].append(pltpu.make_async_copy(x, tokens.at[e * 128:(e + 1) * 128, :], sems.at[e]))
    for k, weight in enumerate((gate, up, down)):
        for i in range(16):
            rows = pl.ds(pl.multiple_of(place[i] * ROWS, 16), ROWS)
            at = (3 * (i % 2) + k) * ROWS
            copies[k].append(pltpu.make_async_copy(pieces[i // 2].at[at:at + ROWS, :], weight.at[rows, :],
                                                   sems.at[4 + 16 * k + i]))
    for copy in copies[0]:
        copy.start()
    chunks = [slice(j * 256, min((j + 1) * 256, FF_DEV)) for j in range(5)]
    for copy in copies[0]:
        copy.wait()
    for copy in copies[1]:
        copy.start()
    for cols in chunks:
        one = jnp.dot(tokens[...], gate[:, cols], preferred_element_type=F32)
        acted[:, cols] = one / (1.0 + jnp.exp(-one))
    for copy in copies[1]:
        copy.wait()
    for copy in copies[2]:
        copy.start()
    for cols in chunks:
        two = jnp.dot(tokens[...], up[:, cols], preferred_element_type=F32)
        hidden[:, cols] = (acted[:, cols] * two).astype(BF16)
    for copy in copies[2]:
        copy.wait()
    stores = []
    for n in range(D // 256):
        rows = slice(n * 256, (n + 1) * 256)
        part = lax.dot_general(hidden[...], down[rows, :], (((1,), (1,)), ((), ())),
                               preferred_element_type=F32).astype(BF16)
        tokens[:, rows] = part
        for e, out in enumerate(outs):
            stores.append(pltpu.make_async_copy(tokens.at[e * 128:(e + 1) * 128, rows], out.at[:, rows],
                                                sems.at[4 * n + e]))
            stores[-1].start()
    for store in stores:
        store.wait()


def feed(xs, pieces):
    return pl.pallas_call(
        feed_body,
        out_shape=(jax.ShapeDtypeStruct((4 * OWN, D), BF16),) * 4,
        in_specs=[hbm_spec()] * 12,
        out_specs=(hbm_spec(),) * 4,
        scratch_shapes=[pltpu.VMEM((512, D), BF16), pltpu.VMEM((D, FF_DEV), BF16), pltpu.VMEM((D, FF_DEV), BF16),
                        pltpu.VMEM((D, FF_DEV), BF16), pltpu.VMEM((512, FF_DEV), BF16), pltpu.VMEM((512, FF_DEV), F32),
                        pltpu.SemaphoreType.DMA((52,))],
        compiler_params=params(60),
        name="feed",
    )(*xs, *pieces)


def fold_body(p0, p1, p2, p3, own, s1, s2, s3):
    for d, out in enumerate((own, s1, s2, s3)):
        rows = slice(d * OWN, (d + 1) * OWN)
        total = p0[rows, :].astype(F32) + p1[rows, :].astype(F32)
        out[...] = (total + p2[rows, :].astype(F32) + p3[rows, :].astype(F32)).astype(out.dtype)


def fold(parts):
    piece = jax.ShapeDtypeStruct((OWN, D), BF16)
    return pl.pallas_call(
        fold_body,
        out_shape=(jax.ShapeDtypeStruct((OWN, D), F32), piece, piece, piece),
        in_specs=[vmem_spec()] * 4,
        out_specs=(vmem_spec(),) * 4,
        compiler_params=params(12),
        name="fold",
    )(*parts)


def finish_body(picked, attention, gate, own, r1, r2, r3, out):
    total = attention[...] + own[...]
    total = total + r1[...].astype(F32) + r2[...].astype(F32) + r3[...].astype(F32)
    out[...] = (picked[...].astype(F32) + gate[...] * total).astype(BF16)


def finish(picked, attention, gate, parts):
    return pl.pallas_call(
        finish_body,
        out_shape=jax.ShapeDtypeStruct((OWN, D), BF16),
        in_specs=[vmem_spec()] * 7,
        out_specs=vmem_spec(),
        compiler_params=params(12),
        name="finish",
    )(picked, attention, gate, *parts)


def merge_body(first, second, out, sems):
    copies = [pltpu.make_async_copy(ref, out.at[s * 3 * ROWS:(s + 1) * 3 * ROWS, :], sems.at[s])
              for s, ref in enumerate((first, second))]
    for copy in copies:
        copy.start()
    for copy in copies:
        copy.wait()


def merge(first, second):
    return pl.pallas_call(
        merge_body,
        out_shape=jax.ShapeDtypeStruct((6 * ROWS, FF_DEV), BF16),
        in_specs=[hbm_spec()] * 2,
        out_specs=vmem_spec(),
        scratch_shapes=[pltpu.SemaphoreType.DMA((2,))],
        compiler_params=params(60),
        name="merge",
    )(first, second)


def join_body(*refs):
    for i, ref in enumerate(refs[:4]):
        refs[4][i * OWN:(i + 1) * OWN, :] = ref[...]


def join(pieces):
    return pl.pallas_call(
        join_body,
        out_shape=jax.ShapeDtypeStruct((4 * OWN, D), BF16),
        in_specs=[vmem_spec()] * 4,
        out_specs=vmem_spec(),
        compiler_params=params(12),
        name="join",
    )(*pieces)


def hold_body(block, out, sem):
    copy = pltpu.make_async_copy(block, out, sem)
    copy.start()
    copy.wait()


def hold(block):
    return pl.pallas_call(
        hold_body,
        out_shape=jax.ShapeDtypeStruct((SEQ_DEV, D), BF16),
        in_specs=[hbm_spec()],
        out_specs=vmem_spec(),
        scratch_shapes=[pltpu.SemaphoreType.DMA],
        compiler_params=params(20),
        name="hold",
    )(block)


def place_body(occupied, chosen, block, *refs):
    pieces = refs[:2]
    out = refs[2]
    rows = refs[3]

    @pl.when(pl.program_id(0) == 0)
    def _():
        for core, piece in enumerate(pieces):
            for dx in range(4):
                at = lax.rem(lax.axis_index("c") + core, 2) * 128 + lax.rem(lax.axis_index("x") + 4 - dx, 4) * OWN
                rows[pl.ds(pl.multiple_of(at, OWN), OWN), :] = piece[dx * OWN:(dx + 1) * OWN, :]

    position = lax.broadcasted_iota(jnp.int32, (STEP, CAP), 0) + pl.program_id(0) * STEP
    slot = lax.broadcasted_iota(jnp.int32, (STEP, CAP), 1)
    hit = jnp.where((position == chosen[...]) & (slot < occupied[0]), 1.0, 0.0)
    taken = jnp.sum(hit, axis=1, keepdims=True) > 0.5
    hit = hit.astype(BF16)
    for n in range(D // 256):
        cols = slice(n * 256, (n + 1) * 256)
        new = jnp.dot(hit, rows[:, cols], preferred_element_type=F32).astype(BF16)
        out[:, cols] = jnp.where(taken, new, block[:, cols])


def put_back(occupied, chosen, block, pieces):
    return pl.pallas_call(
        place_body,
        grid=(SEQ_DEV // STEP,),
        out_shape=jax.ShapeDtypeStruct((SEQ_DEV, D), BF16),
        in_specs=[smem_spec(), pl.BlockSpec((1, CAP), lambda i: (0, 0)),
                  pl.BlockSpec((STEP, D), lambda i: (i, 0))]
        + [pl.BlockSpec((128, D), lambda i: (0, 0))] * 2,
        out_specs=pl.BlockSpec((STEP, D), lambda i: (i, 0)),
        scratch_shapes=[pltpu.VMEM((CAP, D), BF16)],
        compiler_params=params(20),
        name="put_back",
    )(occupied, chosen, block, *pieces)


def shift(value, axis, step, size=4):
    return lax.ppermute(value, axis, [(i, (i + step) % size) for i in range(size)])


def cross(value, step, first):
    pairs = []
    for y in range(4):
        for x in range(4):
            for c in range(2):
                along_x = (c == 0) == first
                to_y, to_x = (y, (x + step) % 4) if along_x else ((y + step) % 4, x)
                pairs.append((8 * y + 2 * x + c, 8 * to_y + 2 * to_x + c))
    return lax.ppermute(value, ("y", "x", "c"), pairs)


def around(value, step):
    pairs = [(2 * z + c, 2 * ((z + (step if c == 0 else 4 - step)) % 4) + c) for z in range(4) for c in range(2)]
    return lax.ppermute(value, ("z", "c"), pairs)


def swap(value):
    return shift(value, "c", 1, 2)


def weight_pairs(s):
    return [(2 * sy + sc, 2 * (2 * sc + (sy + s) % 2) + sy // 2) for sy in range(4) for sc in range(2)]


def tie(*values):
    return lax.optimization_barrier(values)


def local(block, preference, chosen, occupied, gain1, wq, wk, wv, wo, sharpness, gain2, gate_w, up_w, down_w):
    y, z, x, c = (lax.axis_index(n) for n in ("y", "z", "x", "c"))
    own_at = c * 128 + x * OWN
    frequency = 10000.0 ** (-(np.arange(HD) % (HD // 2)) / (HD // 2))
    frequency = jnp.asarray(frequency.astype(np.float32)[None, :])
    packs = pack(gate_w, up_w, down_w)
    *packs, occupied = tie(*packs, occupied)
    got = [lax.ppermute(p, ("y", "c"), weight_pairs(s)) for s, p in enumerate(packs)]
    q, kv, picked = begin(occupied, block, chosen[None, :], gain1[None, :], frequency, wq, wk, wv)

    kv = lax.all_to_all(kv, "z", 0, 0)
    asked = [shift(q, "y", d) for d in (1, 2, 3)]
    merged = merge(*got)
    kv, *asked, merged = tie(kv, *asked, merged)
    near = around(merged, 1)

    scale = sharpness * (LOG2E / math.sqrt(HD))
    parts = []
    for d in (1, 2, 3):
        at = jnp.broadcast_to(jnp.where((y - d) % 4 > y, CAP, -CAP), (4,)).astype(jnp.int32)
        parts.append(shift(attend(False, at, scale, asked[d - 1], kv), "y", 4 - d))
    at = jnp.stack([jnp.where(j < z, CAP, jnp.where(j == z, 0, -CAP)) for j in range(4)]).astype(jnp.int32)
    parts.append(attend(True, at, scale, q, kv))

    *parts, near, merged = tie(*parts, near, merged)
    side, far = around(merged, 3), around(near, 1)
    keep, send = mix(parts, wo)
    others = [swap(piece) for piece in (merged, near, side)]
    met, others[0] = tie(swap(send), others[0])
    own, s1, s2, s3 = split(keep, met)
    moved = [shift(s, "x", d) for d, s in ((1, s1), (2, s2), (3, s3))]
    *moved, others[1] = tie(*moved, others[1])
    attention, normed = middle(picked, own, moved, gain2[None, :])

    moved = [cross(normed, d, True) for d in (1, 2, 3)]
    *moved, side = tie(*moved, side)
    others[2] = swap(side)
    row = join([normed] + moved)
    xs = [row] + [cross(row, e, False) for e in (1, 2, 3)]
    *xs, others[2], far = tie(*xs, others[2], far)
    others.append(swap(far))
    outs = feed(xs, [merged, near, side, far] + others)
    own, s1, s2, s3 = fold([outs[0]] + [cross(outs[e], 4 - e, False) for e in (1, 2, 3)])
    outs = [own] + [cross(s, 4 - d, True) for d, s in ((1, s1), (2, s2), (3, s3))]

    mine = lax.dynamic_slice_in_dim(chosen, own_at, OWN, 0)
    hit = mine[:, None] == jnp.arange(SEQ_DEV, dtype=jnp.int32)[None, :]
    router = jax.nn.sigmoid(jnp.sum(jnp.where(hit, preference[None, :], 0.0), axis=1, keepdims=True))
    result = finish(picked, attention, router, outs)
    *rows, block = tie(*[shift(result, "x", d) for d in (1, 2, 3)], hold(block))
    rows = join([result] + rows)
    return put_back(occupied, chosen[None, :], block, [rows, swap(rows)])


def solution(mesh):
    grid = Mesh(mesh.devices.reshape(4, 4, 4, 2), ("y", "z", "x", "c"))
    ctx, mp = ("y", "z"), ("x", "c")
    return jax.shard_map(
        local,
        mesh=grid,
        in_specs=(P(ctx, None), P(ctx), P(ctx), P(ctx), P(), P(None, mp), P(None, mp), P(None, mp),
                  P(mp, None), P(mp), P(), P(ctx, mp), P(ctx, mp), P(ctx, mp)),
        out_specs=P(ctx, None),
        check_vma=False,
    )
```
